128 devices in a mesh: ctx: 32 (over y, x, core), rows: 4 (over z).
Axes of the slice: x: 4, y: 4, z: 4, core: 2. Of those that a mesh axis runs over, the one named last changes fastest.
Arguments:
- queries: bfloat16 [64, 8192], P('rows', 'ctx'), may hold values from -200 to 200
- keys: bfloat16 [64, 8192, 1024], P('rows', 'ctx'), may hold values from -6 to 6
- values: bfloat16 [64, 8192, 1024], P('rows', 'ctx'), may hold values from -6 to 6
- codes: int32 [64, 8192, 128], P('rows', 'ctx'), may hold values from 0 to 255
- codebook: bfloat16 [8, 16, 256, 8], replicated, may hold values from -15 to 15
- lengths: int32 [64], P('rows'), may hold values from 1024 to 8192, as said below
- blocks: int32 [64, 8, 16], P('rows'), may hold values from 0 to 127, as said below
Outputs:
- attended: bfloat16 [64, 8192], P('rows', 'ctx')
- approx_mass: float32 [64, 64], P('rows', 'ctx')
The draws below stay inside these ranges and needn't reach their ends.
Inputs may be any that keep to these rules, and one draw needn't show every extreme that they name: `lengths`: row 0 has the whole context. Each row and key-value head names 16 different blocks, each holding some position below the row's length.
All inputs are finite; a program needn't handle non-finite values.
Results may differ from the reference program's by a relative error of at most 0.02.
Values may be sent and summed in bfloat16 or wider, within the bound.
A program may use at most 128 MiB of HBM per device.

```python
import jax
import jax.numpy as jnp
from jax import lax

H = 64
KVH = 8
HD = 128
M = 16
CODES = 256
BLK = 64
SEL = 16
SUB = 8
ROWS = 64
CTXT = 8192
NBLK = 128


def shared_lists(key):
    length_key = jax.random.fold_in(key, 11)
    row_lengths = jax.random.randint(length_key, (ROWS,), SEL * BLK, CTXT + 1)
    row_lengths = row_lengths.at[0].set(CTXT)
    order_key = jax.random.fold_in(key, 12)
    random_rank = jax.random.randint(order_key, (ROWS, KVH, NBLK), 0, 1048576)
    ranked_values = random_rank * NBLK + jnp.arange(NBLK, dtype=jnp.int32)[None, None, :]
    usable = (row_lengths + BLK - 1) // BLK
    ranked_values = jnp.where(jnp.arange(NBLK, dtype=jnp.int32)[None, None, :] < usable[:, None, None], ranked_values, -1)
    ignored, chosen = lax.top_k(ranked_values, SEL)
    return (row_lengths.astype(jnp.int32), chosen.astype(jnp.int32))


def draw_lengths(key, part):
    return shared_lists(key)[0]


def draw_blocks(key, part):
    return shared_lists(key)[1]


def draw_queries(key, part):
    key = jax.random.fold_in(key, 5)
    sample = jax.random.truncated_normal(key, -5.0, 5.0, (ROWS, H * HD), jnp.float32)
    return sample.astype(jnp.bfloat16)


def with_ends(result, stream_key, least, largest):
    index_at = [jax.random.randint(jax.random.fold_in(stream_key, axis), (), 0, length) for axis, length in enumerate(result.shape)]
    longest = result.shape.index(max(result.shape))
    neighbour = index_at[:longest] + [(index_at[longest] + 1) % result.shape[longest]] + index_at[longest + 1:]
    return result.at[tuple(index_at)].set(least).at[tuple(neighbour)].set(largest)


def level_of(own_key, shape, split, smallest, largest):
    gain = 1.0
    for dim, shards_of in split:
        draws = jax.random.uniform(jax.random.fold_in(jax.random.fold_in(own_key, 6), dim), (shards_of,), jnp.float32, smallest / len(split), largest / len(split))
        gain = gain * jnp.repeat(jnp.exp(draws), shape[dim] // shards_of).reshape((-1,) + (1,) * (len(shape) - 1 - dim))
    return gain


def scatter_about(key, extent, spread, most, cuts=(), kind=jnp.bfloat16):
    drawn = jax.random.normal(key, extent, jnp.float32) * spread
    if len(cuts) > 0:
        drawn = level_of(key, extent, cuts, -0.22, 0.18) * drawn
    return jnp.clip(drawn, min=-most, max=most).astype(kind)


def setup_inputs(seed: int = 0) -> dict:
    key_of = jax.random.split(jax.random.key(seed), 8)
    return {
        "queries": draw_queries(jax.random.fold_in(key_of[7], 71), 0),
        "keys": scatter_about(key_of[1], (ROWS, CTXT, KVH * HD), 1.0, 6.0, ((0, 4), (1, 32))),
        "values": scatter_about(key_of[2], (ROWS, CTXT, KVH * HD), 1.0, 6.0, ((0, 4), (1, 32))),
        "codes": with_ends(jax.random.randint(key_of[3], (ROWS, CTXT, KVH * M), 0, CODES), jax.random.fold_in(key_of[3], 1), 0, CODES - 1).astype(jnp.int32),
        "codebook": scatter_about(key_of[4], (KVH, M, CODES, SUB), 3.0, 15.0),
        "lengths": draw_lengths(jax.random.fold_in(key_of[7], 71), 0),
        "blocks": draw_blocks(jax.random.fold_in(key_of[7], 71), 0),
    }


NEGATIVE = -1e30


def reference(queries, keys, values, codes, codebook, lengths, blocks):
    score_scale = HD ** -0.5
    groups = H // KVH
    book_wide = codebook.astype(jnp.float32)

    def one_row(row_items):
        query_row, key_rows, value_rows, code_rows, length, chosen = row_items
        query_f = query_row.astype(jnp.float32)
        split_query = query_f.reshape(KVH, groups, M, HD // M)
        lookup = (jnp.einsum('gjms,gmcs->gjmc', split_query, book_wide) * score_scale).astype(jnp.bfloat16)
        lookup = lax.optimization_barrier(lookup).astype(jnp.float32)
        code_index = code_rows.reshape(CTXT, KVH, M)
        picked = lookup[jnp.arange(KVH)[None, :, None], :, jnp.arange(M)[None, None, :], code_index]
        approx = jnp.transpose(jnp.sum(picked, axis=2), (1, 2, 0))
        position = jnp.arange(CTXT, dtype=jnp.int32)
        inside = position < length
        masked = jnp.where(inside[None, None, :], approx, NEGATIVE)
        peak = jnp.max(masked, axis=-1)
        denominator = jnp.sum(jnp.where(inside[None, None, :], jnp.exp(approx - peak[..., None]), 0.0), axis=-1)
        log_mass = (peak + jnp.log(denominator)).reshape(H)
        key_heads = key_rows.astype(jnp.float32).reshape(CTXT, KVH, HD)
        value_heads = value_rows.astype(jnp.float32).reshape(CTXT, KVH, HD)
        scores = jnp.einsum('gjd,tgd->gjt', query_f.reshape(KVH, groups, HD), key_heads) * score_scale
        block_of = position // BLK
        chosen_mask = jnp.any(chosen[:, :, None] == block_of[None, None, :], axis=1)
        used = (chosen_mask & inside[None, :])[:, None, :]
        peak_att = jnp.max(jnp.where(used, scores, NEGATIVE), axis=-1)
        weights = jnp.where(used, jnp.exp(scores - peak_att[..., None]), 0.0)
        denom_att = jnp.sum(weights, axis=-1)
        rounded = lax.optimization_barrier(weights.astype(jnp.bfloat16)).astype(jnp.float32)
        weighted = jnp.einsum('gjt,tgd->gjd', rounded, value_heads)
        attended = (weighted / denom_att[..., None]).reshape(H * HD).astype(jnp.bfloat16)
        return attended, log_mass

    attended, approx_mass = lax.map(one_row, (queries, keys, values, codes, lengths, blocks))
    return attended, approx_mass
```

```python
import functools

import jax
import jax.numpy as jnp
from jax import lax
from jax.experimental import pallas as pl
from jax.experimental.pallas import tpu as pltpu
from jax.sharding import PartitionSpec as P

H = 64
KVH = 8
HD = 128
M = 16
CODES = 256
BLK = 64
SEL = 16
N = 32
R = 16
T = 256
PAIRS = 4
NEGATIVE = -1e30
SCALE = HD ** (-0.5)
F32 = jnp.float32
BF16 = jnp.bfloat16
MESH = pl.DeviceIdType.MESH


def iota(shape, dim):
    return lax.broadcasted_iota(jnp.int32, shape, dim)


def take(table, index):
    return jnp.take_along_axis(table, index, axis=1, mode="promise_in_bounds")


def kernel(
    q_hbm, k_hbm, v_hbm, c_hbm, cb_hbm, len_hbm, blk_hbm,
    att_ref, mass_ref,
    qbuf, qf0, qf1, qp0, qp1, codes, keys, vals, cb, raw_lo, raw_hi, tab_lo, tab_hi,
    khat, lens, blk, chosen, idx_a, idx_b, guesses, scores, weights, stage, sendbuf, recvbuf, stat, stat_out, stat_in,
    q_own, small_sem, code_sem, key_sem, val_sem,
    q_send, q_recv, o_send, o_recv, s_send, s_recv,
):
    me = lax.axis_index("ctx")

    own_q = pltpu.make_async_copy(q_hbm, q_own, small_sem.at[0])
    book = pltpu.make_async_copy(cb_hbm, cb, small_sem.at[1])
    lengths = pltpu.make_async_copy(len_hbm, lens, small_sem.at[2])
    selected = pltpu.make_async_copy(blk_hbm, blk, small_sem.at[3])
    for copy in (own_q, book, lengths, selected):
        copy.start()

    def copy_of(source, target, sem, r):
        return pltpu.make_async_copy(source.at[r], target.at[r], sem.at[r])

    def start_rows(source, target, sem):
        def step(r, carry):
            copy_of(source, target, sem, r).start()
            return carry

        lax.fori_loop(0, R, step, 0)

    start_rows(c_hbm, codes, code_sem)

    barrier = pltpu.get_barrier_semaphore()

    def greet(k, carry):
        pl.semaphore_signal(
            barrier, inc=1, device_id={"ctx": lax.rem(me + k, N)}, device_id_type=MESH
        )
        return carry

    lax.fori_loop(1, N, greet, 0)
    start_rows(k_hbm, keys, key_sem)
    start_rows(v_hbm, vals, val_sem)
    own_q.wait()
    qbuf[me] = q_own[...]
    pl.semaphore_wait(barrier, N - 1)

    def send_query(k, carry):
        pltpu.make_async_remote_copy(
            src_ref=q_own,
            dst_ref=qbuf.at[me],
            send_sem=q_send,
            recv_sem=q_recv,
            device_id={"ctx": lax.rem(me + k, N)},
            device_id_type=MESH,
        ).start()
        return carry

    lax.fori_loop(1, N, send_query, 0)

    book.wait()

    def widen(i, carry):
        rows = pl.ds(pl.multiple_of(i * 64, 64), 64)
        wide = cb[rows, :].astype(F32)
        raw_lo[rows, :] = wide[:, :128]
        raw_hi[rows, :] = wide[:, 128:]
        for s in range(8):
            spread = pl.ds(i * 64 + s, 8, stride=8)
            packed = pl.ds(pl.multiple_of(i * 64 + s * 8, 8), 8)
            tab_lo[packed, :] = raw_lo[spread, :]
            tab_hi[packed, :] = raw_hi[spread, :]
        return carry

    lax.fori_loop(0, 16, widen, 0)

    lengths.wait()
    selected.wait()
    names = blk[...].reshape(R * KVH, SEL)
    total = jnp.zeros((R * KVH, T), F32)
    for b in range(T // BLK):
        hit = (names == me * (T // BLK) + b).astype(F32).astype(BF16)
        spot = (iota((SEL, T), 1) // BLK == b).astype(F32).astype(BF16)
        total = total + jnp.dot(hit, spot, preferred_element_type=F32)
    chosen[...] = total

    def decode_row(r, index):
        for i in range(16):
            columns = []
            code = index[i * 8 : i * 8 + 8, :]
            for half in range(2):
                part = code[:, half * 128 : half * 128 + 128]
                low = part & 127
                high = part > 127
                parts = []
                for s in range(8):
                    at = (i * 8 + s) * 8
                    parts.append(
                        jnp.where(
                            high, take(tab_hi[at : at + 8, :], low), take(tab_lo[at : at + 8, :], low)
                        )
                    )
                columns.append(jnp.concatenate(parts, axis=0))
            khat[r, i * 64 : i * 64 + 64, :] = jnp.concatenate(columns, axis=1).astype(BF16)

    copy_of(c_hbm, codes, code_sem, 0).wait()
    idx_a[...] = codes[0].T

    def decode_two(n, carry):
        copy_of(c_hbm, codes, code_sem, 2 * n + 1).wait()

        @pl.when(n < R // 2 - 1)
        def _():
            copy_of(c_hbm, codes, code_sem, 2 * n + 2).wait()

        idx_b[...] = codes[2 * n + 1].T
        decode_row(2 * n, idx_a)
        idx_a[...] = codes[jnp.minimum(2 * n + 2, R - 1)].T
        decode_row(2 * n + 1, idx_b)
        return carry

    lax.fori_loop(0, R // 2, decode_two, 0)

    whole = qbuf.at[pl.ds(0, N - 1)]
    pltpu.make_async_copy(whole, whole, q_recv).wait()
    pltpu.make_async_copy(whole, whole, q_send).wait()
    to_row = iota((HD, HD), 0)
    to_col = iota((HD, HD), 1)
    origin = (to_col & 64) | ((to_col & 7) << 3) | ((to_col >> 3) & 7)
    permute = (to_row == origin).astype(F32).astype(BF16)
    for hh, (plain, turned) in enumerate(((qf0, qp0), (qf1, qp1))):
        part = qbuf[:, :, hh * HD : hh * HD + HD].reshape(N * R, HD)
        plain[...] = part.astype(F32)
        turned[...] = jnp.dot(part, permute, preferred_element_type=F32)

    def wait_rows(r, carry):
        copy_of(k_hbm, keys, key_sem, r).wait()
        copy_of(v_hbm, vals, val_sem, r).wait()
        return carry

    lax.fori_loop(0, R, wait_rows, 0)

    left = (iota((16, 1), 0) & 7) < 4
    left_wide = (iota((16, HD), 0) & 7) < 4
    position = iota((1, T), 1) + me * T
    lane = iota((8, 128), 1)

    def spread_heads(part0, part1, r, p):
        at = pl.ds(p * 128 + r, 8, stride=16)
        both = jnp.concatenate([part0[at, :], part1[at, :]], axis=0)
        return jnp.concatenate(
            [jnp.where(left_wide, both, 0.0), jnp.where(left_wide, 0.0, both)], axis=1
        ).astype(BF16)

    def place(n):
        step = n // 4
        turn = jnp.where(lax.rem(me, 2) == 0, step + 1, 3 - step)
        return lax.rem(me // 8 + turn, PAIRS), lax.rem(n, 4) * 4

    def multiply(n):
        p, first = place(n)
        wide = pl.ds(pl.multiple_of(p * 256, 256), 256)
        for u in range(4):
            r = first + u
            at = slice(u * 16, u * 16 + 16)
            guesses[at, :] = jnp.dot(
                spread_heads(qp0, qp1, r, p), khat[r, wide, :], preferred_element_type=F32
            )
            scores[at, :] = lax.dot_general(
                spread_heads(qf0, qf1, r, p),
                keys[r, :, wide],
                (((1,), (1,)), ((), ())),
                preferred_element_type=F32,
            )

    def weigh(n):
        p, first = place(n)
        eight = pl.ds(pl.multiple_of(p * 8, 8), 8)
        kept = stat[eight, :]
        for u in range(4):
            r = first + u
            at = slice(u * 16, u * 16 + 16)
            inside = position < lens[r]
            guess = jnp.where(inside, guesses[at, :] * SCALE, NEGATIVE)
            guess_peak = jnp.max(guess, axis=1, keepdims=True)
            guess_total = jnp.sum(
                jnp.where(inside, jnp.exp(guess - guess_peak), 0.0), axis=1, keepdims=True
            )
            here = chosen[pl.ds(r * KVH + 2 * p, 1), :]
            there = chosen[pl.ds(r * KVH + 2 * p + 1, 1), :]
            used = (jnp.where(left, here, there) > 0.5) & inside
            score = jnp.where(used, scores[at, :] * SCALE, NEGATIVE)
            peak = jnp.max(score, axis=1, keepdims=True)
            weight = jnp.where(used, jnp.exp(score - peak), 0.0)
            weight_total = jnp.sum(weight, axis=1, keepdims=True)
            weights[at, :] = weight.astype(BF16)
            for kind, value in enumerate((guess_peak, guess_total, peak, weight_total)):
                for hh in range(2):
                    kept = jnp.where(
                        lane == kind * 32 + hh * 16 + r, value[hh * 8 : hh * 8 + 8], kept
                    )
        stat[eight, :] = kept

    def average(n):
        p, first = place(n)
        wide = pl.ds(pl.multiple_of(p * 256, 256), 256)
        for u in range(4):
            r = first + u
            summed = jnp.dot(
                weights[u * 16 : u * 16 + 16, :], vals[r, :, wide], preferred_element_type=F32
            )
            summed = jnp.where(left, summed[:, :HD], summed[:, HD:])
            stage[pl.ds(p * 256 + r, 8, stride=32), :] = summed[:8]
            stage[pl.ds(p * 256 + 16 + r, 8, stride=32), :] = summed[8:]

    def send_parts(n):
        p, _ = place(n)
        block = pl.ds(pl.multiple_of(p * 256, 256), 256)
        sendbuf[block, :] = stage[block, :].astype(BF16)
        for k in range(8):
            stat_out[p * 8 + k] = stat[pl.ds(p * 8 + k, 1), :]

        def send_to(k, inner):
            to = p * 8 + k

            @pl.when(to != me)
            def _():
                pltpu.make_async_remote_copy(
                    src_ref=stat_out.at[to],
                    dst_ref=stat_in.at[me],
                    send_sem=s_send,
                    recv_sem=s_recv,
                    device_id={"ctx": to},
                    device_id_type=MESH,
                ).start()
                pltpu.make_async_remote_copy(
                    src_ref=sendbuf.at[pl.ds(pl.multiple_of(to * 32, 32), 32)],
                    dst_ref=recvbuf.at[pl.ds(pl.multiple_of(me * 32, 32), 32)],
                    send_sem=o_send,
                    recv_sem=o_recv,
                    device_id={"ctx": to},
                    device_id_type=MESH,
                ).start()

            return inner

        lax.fori_loop(0, 8, send_to, 0)

    multiply(0)
    weigh(0)
    multiply(1)

    def attend(n, carry):
        average(n - 2)
        weigh(n - 1)
        multiply(n)

        @pl.when(lax.rem(n, 4) == 1)
        def _():
            send_parts(n - 2)

        return carry

    lax.fori_loop(2, R, attend, 0)
    average(R - 2)
    weigh(R - 1)
    average(R - 1)
    send_parts(R - 1)
    mine = pl.ds(pl.multiple_of(me * 32, 32), 32)
    recvbuf[mine, :] = sendbuf[mine, :]
    stat_in[me] = stat_out[me]

    some = stat_in.at[pl.ds(0, N - 1)]
    pltpu.make_async_copy(some, some, s_recv).wait()
    stats = stat_in[...].reshape(N, 128)
    top = jnp.max(stats, axis=0, keepdims=True)
    factor = jnp.exp(stats - top)
    totals = jnp.sum(factor * pltpu.roll(stats, 96, 1), axis=0, keepdims=True)
    mass = top + jnp.log(totals)
    mass_ref[0:1, :] = mass[:, 0:16]
    mass_ref[1:2, :] = mass[:, 16:32]
    share = (factor / totals)[:, 64:96].T
    source = iota((N, N * 32), 1) // 32
    spread = (source == iota((N, N * 32), 0)).astype(F32).astype(BF16)
    mix = jnp.dot(share.astype(BF16), spread, preferred_element_type=F32)
    same = (iota((32, N * 32), 1) & 31) == iota((32, N * 32), 0)
    mix = jnp.where(same, mix, 0.0).astype(BF16)
    some = recvbuf.at[pl.ds(0, (N - 1) * 32)]
    pltpu.make_async_copy(some, some, o_recv).wait()
    result = jnp.dot(mix, recvbuf[...], preferred_element_type=F32)
    att_ref[:, 0:HD] = result[:R].astype(BF16)
    att_ref[:, HD:] = result[R:].astype(BF16)
    some = stat_in.at[pl.ds(0, N - 1)]
    pltpu.make_async_copy(some, some, s_send).wait()
    some = recvbuf.at[pl.ds(0, (N - 1) * 32)]
    pltpu.make_async_copy(some, some, o_send).wait()


def body(queries, keys, values, codes, codebook, lengths, blocks):
    book = codebook.transpose(0, 1, 3, 2).reshape(KVH * M * 8, CODES)
    anywhere = pl.BlockSpec(memory_space=pl.ANY)
    vmem = pl.BlockSpec(memory_space=pltpu.VMEM)
    dma = pltpu.SemaphoreType.DMA
    attended, mass = pl.pallas_call(
        kernel,
        out_shape=(
            jax.ShapeDtypeStruct((R, 2 * HD), BF16),
            jax.ShapeDtypeStruct((2, R), F32),
        ),
        in_specs=[anywhere] * 7,
        out_specs=(vmem, vmem),
        scratch_shapes=[
            pltpu.VMEM((N, R, 2 * HD), BF16),
            pltpu.VMEM((N * R, HD), F32),
            pltpu.VMEM((N * R, HD), F32),
            pltpu.VMEM((N * R, HD), F32),
            pltpu.VMEM((N * R, HD), F32),
            pltpu.VMEM((R, T, KVH * M), jnp.int32),
            pltpu.VMEM((R, T, KVH * HD), BF16),
            pltpu.VMEM((R, T, KVH * HD), BF16),
            pltpu.VMEM((KVH * M * 8, CODES), BF16),
            pltpu.VMEM((KVH * M * 8, 128), F32),
            pltpu.VMEM((KVH * M * 8, 128), F32),
            pltpu.VMEM((KVH * M * 8, 128), F32),
            pltpu.VMEM((KVH * M * 8, 128), F32),
            pltpu.VMEM((R, KVH * HD, T), BF16),
            pltpu.SMEM((R,), jnp.int32),
            pltpu.VMEM((R, KVH, SEL), jnp.int32),
            pltpu.VMEM((R * KVH, T), F32),
            pltpu.VMEM((KVH * M, T), jnp.int32),
            pltpu.VMEM((KVH * M, T), jnp.int32),
            pltpu.VMEM((64, T), F32),
            pltpu.VMEM((64, T), F32),
            pltpu.VMEM((64, T), BF16),
            pltpu.VMEM((N * 32, HD), F32),
            pltpu.VMEM((N * 32, HD), BF16),
            pltpu.VMEM((N * 32, HD), BF16),
            pltpu.VMEM((N, 128), F32),
            pltpu.VMEM((N, 1, 128), F32),
            pltpu.VMEM((N, 1, 128), F32),
            pltpu.VMEM((R, 2 * HD), BF16),
            dma((4,)),
            dma((R,)),
            dma((R,)),
            dma((R,)),
            dma, dma, dma, dma, dma, dma,
        ],
        compiler_params=pltpu.CompilerParams(
            collective_id=0, has_side_effects=True, vmem_limit_bytes=62 * 2**20
        ),
        name="decode_attention",
    )(queries, keys, values, codes, book, lengths, blocks)
    return attended, mass.T


def solution(mesh):
    placed = (
        P("rows", "ctx"),
        P("rows", "ctx", None),
        P("rows", "ctx", None),
        P("rows", "ctx", None),
        P(),
        P("rows"),
        P("rows", None, None),
    )
    return jax.shard_map(
        body,
        mesh=mesh,
        in_specs=placed,
        out_specs=(P("rows", "ctx"), P("rows", "ctx")),
        check_vma=False,
    )
```

```python
import functools

import jax
import jax.numpy as jnp
from jax import lax
from jax.experimental import pallas as pl
from jax.experimental.pallas import tpu as pltpu
from jax.sharding import PartitionSpec as P

H = 64
KVH = 8
HD = 128
M = 16
CODES = 256
BLK = 64
SEL = 16
N = 32
R = 16
T = 256
PAIRS = 4
EARLY = 2
NEGATIVE = -1e30
SCALE = HD ** (-0.5)
F32 = jnp.float32
BF16 = jnp.bfloat16
MESH = pl.DeviceIdType.MESH


def iota(shape, dim):
    return lax.broadcasted_iota(jnp.int32, shape, dim)


def take(table, index):
    return jnp.take_along_axis(table, index, axis=1, mode="promise_in_bounds")


def kernel(
    q_hbm, k_hbm, v_hbm, c_hbm, cb_hbm, len_hbm, blk_hbm,
    att_ref, mass_ref,
    qbuf, qf0, qf1, qp0, qp1, codes, keys, vals, cb, raw_lo, raw_hi, tab_lo, tab_hi,
    khat, lens, blk, chosen, idx_a, idx_b, guesses, scores, weights, stage, sendbuf, recvbuf, stat, stat_out, stat_in,
    q_own, small_sem, code_sem, key_sem, val_sem,
    q_send, q_recv, o_send, o_recv, s_send, s_recv,
):
    me = lax.axis_index("ctx")

    barrier = pltpu.get_barrier_semaphore()

    def greet(k, carry):
        pl.semaphore_signal(
            barrier, inc=1, device_id={"ctx": lax.rem(me + k, N)}, device_id_type=MESH
        )
        return carry

    lax.fori_loop(1, N, greet, 0)

    own_q = pltpu.make_async_copy(q_hbm, q_own, small_sem.at[0])
    book = pltpu.make_async_copy(cb_hbm, cb, small_sem.at[1])
    lengths = pltpu.make_async_copy(len_hbm, lens, small_sem.at[2])
    selected = pltpu.make_async_copy(blk_hbm, blk, small_sem.at[3])

    def two_codes(n):
        rows = pl.ds(2 * n, 2)
        return pltpu.make_async_copy(c_hbm.at[rows], codes.at[rows], code_sem.at[n])

    all_keys = pltpu.make_async_copy(k_hbm, keys, key_sem)
    all_vals = pltpu.make_async_copy(v_hbm, vals, val_sem)
    book.start()
    two_codes(0).start()
    for copy in (own_q, lengths, selected):
        copy.start()
    for n in range(1, R // 2):
        two_codes(n).start()
    all_keys.start()
    all_vals.start()
    own_q.wait()
    qbuf[me] = q_own[...]

    book.wait()

    def widen(i, carry):
        rows = pl.ds(pl.multiple_of(i * 64, 64), 64)
        wide = cb[rows, :].astype(F32)
        raw_lo[rows, :] = wide[:, :128]
        raw_hi[rows, :] = wide[:, 128:]
        for s in range(8):
            spread = pl.ds(i * 64 + s, 8, stride=8)
            packed = pl.ds(pl.multiple_of(i * 64 + s * 8, 8), 8)
            tab_lo[packed, :] = raw_lo[spread, :]
            tab_hi[packed, :] = raw_hi[spread, :]
        return carry

    lax.fori_loop(0, 16, widen, 0)

    lengths.wait()
    selected.wait()
    names = blk[...].reshape(R * KVH, SEL)
    total = jnp.zeros((R * KVH, T), F32)
    for b in range(T // BLK):
        hit = (names == me * (T // BLK) + b).astype(F32).astype(BF16)
        spot = (iota((SEL, T), 1) // BLK == b).astype(F32).astype(BF16)
        total = total + jnp.dot(hit, spot, preferred_element_type=F32)
    chosen[...] = total

    def decode_row(r, index):
        for i in range(16):
            columns = []
            code = index[i * 8 : i * 8 + 8, :]
            for half in range(2):
                part = code[:, half * 128 : half * 128 + 128]
                low = part & 127
                high = part > 127
                parts = []
                for s in range(8):
                    at = (i * 8 + s) * 8
                    parts.append(
                        jnp.where(
                            high, take(tab_hi[at : at + 8, :], low), take(tab_lo[at : at + 8, :], low)
                        )
                    )
                columns.append(jnp.concatenate(parts, axis=0))
            khat[r, i * 64 : i * 64 + 64, :] = jnp.concatenate(columns, axis=1).astype(BF16)

    two_codes(0).wait()
    idx_a[...] = codes[0].T

    def decode_two(n, carry):
        @pl.when(n < R // 2 - 1)
        def _():
            two_codes(n + 1).wait()

        idx_b[...] = codes[2 * n + 1].T
        decode_row(2 * n, idx_a)
        idx_a[...] = codes[jnp.minimum(2 * n + 2, R - 1)].T
        decode_row(2 * n + 1, idx_b)
        return carry

    lax.fori_loop(0, EARLY, decode_two, 0)
    pl.semaphore_wait(barrier, N - 1)

    def send_query(k, carry):
        pltpu.make_async_remote_copy(
            src_ref=q_own,
            dst_ref=qbuf.at[me],
            send_sem=q_send,
            recv_sem=q_recv,
            device_id={"ctx": lax.rem(me + k, N)},
            device_id_type=MESH,
        ).start()
        return carry

    lax.fori_loop(1, N, send_query, 0)

    lax.fori_loop(EARLY, R // 2, decode_two, 0)

    whole = qbuf.at[pl.ds(0, N - 1)]
    pltpu.make_async_copy(whole, whole, q_recv).wait()
    pltpu.make_async_copy(whole, whole, q_send).wait()
    to_row = iota((HD, HD), 0)
    to_col = iota((HD, HD), 1)
    origin = (to_col & 64) | ((to_col & 7) << 3) | ((to_col >> 3) & 7)
    permute = (to_row == origin).astype(F32).astype(BF16)
    for hh, (plain, turned) in enumerate(((qf0, qp0), (qf1, qp1))):
        part = qbuf[:, :, hh * HD : hh * HD + HD].reshape(N * R, HD)
        plain[...] = part.astype(F32)
        turned[...] = jnp.dot(part, permute, preferred_element_type=F32)

    all_keys.wait()
    all_vals.wait()
    left = (iota((16, 1), 0) & 7) < 4
    left_wide = (iota((16, HD), 0) & 7) < 4
    position = iota((1, T), 1) + me * T
    lane = iota((8, 128), 1)

    def spread_heads(part0, part1, r, p):
        at = pl.ds(p * 128 + r, 8, stride=16)
        both = jnp.concatenate([part0[at, :], part1[at, :]], axis=0)
        return jnp.concatenate(
            [jnp.where(left_wide, both, 0.0), jnp.where(left_wide, 0.0, both)], axis=1
        ).astype(BF16)

    def place(n):
        step = n // 4
        turn = jnp.where(lax.rem(me, 2) == 0, step + 1, 3 - step)
        return lax.rem(me // 8 + turn, PAIRS), lax.rem(n, 4) * 4

    def multiply(n):
        p, first = place(n)
        wide = pl.ds(pl.multiple_of(p * 256, 256), 256)
        for u in range(4):
            r = first + u
            at = slice(u * 16, u * 16 + 16)
            guesses[at, :] = jnp.dot(
                spread_heads(qp0, qp1, r, p), khat[r, wide, :], preferred_element_type=F32
            )
            scores[at, :] = lax.dot_general(
                spread_heads(qf0, qf1, r, p),
                keys[r, :, wide],
                (((1,), (1,)), ((), ())),
                preferred_element_type=F32,
            )

    def weigh(n):
        p, first = place(n)
        eight = pl.ds(pl.multiple_of(p * 8, 8), 8)
        kept = stat[eight, :]
        for u in range(4):
            r = first + u
            at = slice(u * 16, u * 16 + 16)
            inside = position < lens[r]
            guess = jnp.where(inside, guesses[at, :] * SCALE, NEGATIVE)
            guess_peak = jnp.max(guess, axis=1, keepdims=True)
            guess_total = jnp.sum(
                jnp.where(inside, jnp.exp(guess - guess_peak), 0.0), axis=1, keepdims=True
            )
            here = chosen[pl.ds(r * KVH + 2 * p, 1), :]
            there = chosen[pl.ds(r * KVH + 2 * p + 1, 1), :]
            used = (jnp.where(left, here, there) > 0.5) & inside
            score = jnp.where(used, scores[at, :] * SCALE, NEGATIVE)
            peak = jnp.max(score, axis=1, keepdims=True)
            weight = jnp.where(used, jnp.exp(score - peak), 0.0)
            weight_total = jnp.sum(weight, axis=1, keepdims=True)
            weights[at, :] = weight.astype(BF16)
            for kind, value in enumerate((guess_peak, guess_total, peak, weight_total)):
                for hh in range(2):
                    kept = jnp.where(
                        lane == kind * 32 + hh * 16 + r, value[hh * 8 : hh * 8 + 8], kept
                    )
        stat[eight, :] = kept

    def average(n):
        p, first = place(n)
        wide = pl.ds(pl.multiple_of(p * 256, 256), 256)
        for u in range(4):
            r = first + u
            summed = jnp.dot(
                weights[u * 16 : u * 16 + 16, :], vals[r, :, wide], preferred_element_type=F32
            )
            summed = jnp.where(left, summed[:, :HD], summed[:, HD:])
            stage[pl.ds(p * 256 + r, 8, stride=32), :] = summed[:8]
            stage[pl.ds(p * 256 + 16 + r, 8, stride=32), :] = summed[8:]

    def send_parts(n):
        p, _ = place(n)
        block = pl.ds(pl.multiple_of(p * 256, 256), 256)
        sendbuf[block, :] = stage[block, :].astype(BF16)
        for k in range(8):
            stat_out[p * 8 + k] = stat[pl.ds(p * 8 + k, 1), :]

        def send_to(k, inner):
            to = p * 8 + k

            @pl.when(to != me)
            def _():
                pltpu.make_async_remote_copy(
                    src_ref=stat_out.at[to],
                    dst_ref=stat_in.at[me],
                    send_sem=s_send,
                    recv_sem=s_recv,
                    device_id={"ctx": to},
                    device_id_type=MESH,
                ).start()
                pltpu.make_async_remote_copy(
                    src_ref=sendbuf.at[pl.ds(pl.multiple_of(to * 32, 32), 32)],
                    dst_ref=recvbuf.at[pl.ds(pl.multiple_of(me * 32, 32), 32)],
                    send_sem=o_send,
                    recv_sem=o_recv,
                    device_id={"ctx": to},
                    device_id_type=MESH,
                ).start()

            return inner

        lax.fori_loop(0, 8, send_to, 0)

    multiply(0)
    weigh(0)
    multiply(1)

    def attend(n, carry):
        average(n - 2)
        weigh(n - 1)
        multiply(n)

        @pl.when(lax.rem(n, 4) == 1)
        def _():
            send_parts(n - 2)

        return carry

    lax.fori_loop(2, R, attend, 0)
    average(R - 2)
    weigh(R - 1)
    average(R - 1)
    send_parts(R - 1)
    mine = pl.ds(pl.multiple_of(me * 32, 32), 32)
    recvbuf[mine, :] = sendbuf[mine, :]
    stat_in[me] = stat_out[me]

    some = stat_in.at[pl.ds(0, N - 1)]
    pltpu.make_async_copy(some, some, s_recv).wait()
    stats = stat_in[...].reshape(N, 128)
    top = jnp.max(stats, axis=0, keepdims=True)
    factor = jnp.exp(stats - top)
    totals = jnp.sum(factor * pltpu.roll(stats, 96, 1), axis=0, keepdims=True)
    mass = top + jnp.log(totals)
    mass_ref[0:1, :] = mass[:, 0:16]
    mass_ref[1:2, :] = mass[:, 16:32]
    share = (factor / totals)[:, 64:96].T
    source = iota((N, N * 32), 1) // 32
    spread = (source == iota((N, N * 32), 0)).astype(F32).astype(BF16)
    mix = jnp.dot(share.astype(BF16), spread, preferred_element_type=F32)
    same = (iota((32, N * 32), 1) & 31) == iota((32, N * 32), 0)
    mix = jnp.where(same, mix, 0.0).astype(BF16)
    some = recvbuf.at[pl.ds(0, (N - 1) * 32)]
    pltpu.make_async_copy(some, some, o_recv).wait()
    result = jnp.dot(mix, recvbuf[...], preferred_element_type=F32)
    att_ref[:, 0:HD] = result[:R].astype(BF16)
    att_ref[:, HD:] = result[R:].astype(BF16)
    some = stat_in.at[pl.ds(0, N - 1)]
    pltpu.make_async_copy(some, some, s_send).wait()
    some = recvbuf.at[pl.ds(0, (N - 1) * 32)]
    pltpu.make_async_copy(some, some, o_send).wait()


def body(queries, keys, values, codes, codebook, lengths, blocks):
    book = codebook.transpose(0, 1, 3, 2).reshape(KVH * M * 8, CODES)
    anywhere = pl.BlockSpec(memory_space=pl.ANY)
    vmem = pl.BlockSpec(memory_space=pltpu.VMEM)
    dma = pltpu.SemaphoreType.DMA
    attended, mass = pl.pallas_call(
        kernel,
        out_shape=(
            jax.ShapeDtypeStruct((R, 2 * HD), BF16),
            jax.ShapeDtypeStruct((2, R), F32),
        ),
        in_specs=[anywhere] * 7,
        out_specs=(vmem, vmem),
        scratch_shapes=[
            pltpu.VMEM((N, R, 2 * HD), BF16),
            pltpu.VMEM((N * R, HD), F32),
            pltpu.VMEM((N * R, HD), F32),
            pltpu.VMEM((N * R, HD), F32),
            pltpu.VMEM((N * R, HD), F32),
            pltpu.VMEM((R, T, KVH * M), jnp.int32),
            pltpu.VMEM((R, T, KVH * HD), BF16),
            pltpu.VMEM((R, T, KVH * HD), BF16),
            pltpu.VMEM((KVH * M * 8, CODES), BF16),
            pltpu.VMEM((KVH * M * 8, 128), F32),
            pltpu.VMEM((KVH * M * 8, 128), F32),
            pltpu.VMEM((KVH * M * 8, 128), F32),
            pltpu.VMEM((KVH * M * 8, 128), F32),
            pltpu.VMEM((R, KVH * HD, T), BF16),
            pltpu.SMEM((R,), jnp.int32),
            pltpu.VMEM((R, KVH, SEL), jnp.int32),
            pltpu.VMEM((R * KVH, T), F32),
            pltpu.VMEM((KVH * M, T), jnp.int32),
            pltpu.VMEM((KVH * M, T), jnp.int32),
            pltpu.VMEM((64, T), F32),
            pltpu.VMEM((64, T), F32),
            pltpu.VMEM((64, T), BF16),
            pltpu.VMEM((N * 32, HD), F32),
            pltpu.VMEM((N * 32, HD), BF16),
            pltpu.VMEM((N * 32, HD), BF16),
            pltpu.VMEM((N, 128), F32),
            pltpu.VMEM((N, 1, 128), F32),
            pltpu.VMEM((N, 1, 128), F32),
            pltpu.VMEM((R, 2 * HD), BF16),
            dma((4,)),
            dma((R // 2,)),
            dma, dma,
            dma, dma, dma, dma, dma, dma,
        ],
        compiler_params=pltpu.CompilerParams(
            collective_id=0, has_side_effects=True, vmem_limit_bytes=62 * 2**20
        ),
        name="decode_attention",
    )(queries, keys, values, codes, book, lengths, blocks)

    def hand_over(from_attended, from_mass, to_attended, to_mass, sems):
        first = pltpu.make_async_copy(from_attended, to_attended, sems.at[0])
        second = pltpu.make_async_copy(from_mass, to_mass, sems.at[1])
        first.start()
        second.start()
        first.wait()
        second.wait()

    attended, mass = pl.pallas_call(
        hand_over,
        out_shape=(
            jax.ShapeDtypeStruct((R, 2 * HD), BF16),
            jax.ShapeDtypeStruct((2, R), F32),
        ),
        in_specs=[anywhere] * 2,
        out_specs=(anywhere, anywhere),
        scratch_shapes=[dma((2,))],
        name="hand_over",
    )(attended, mass)
    return attended, mass.T


def solution(mesh):
    placed = (
        P("rows", "ctx"),
        P("rows", "ctx", None),
        P("rows", "ctx", None),
        P("rows", "ctx", None),
        P(),
        P("rows"),
        P("rows", None, None),
    )
    return jax.shard_map(
        body,
        mesh=mesh,
        in_specs=placed,
        out_specs=(P("rows", "ctx"), P("rows", "ctx")),
        check_vma=False,
    )
```

```python
import functools

import jax
import jax.numpy as jnp
from jax import lax
from jax.experimental import pallas as pl
from jax.experimental.pallas import tpu as pltpu
from jax.sharding import PartitionSpec as P

H = 64
KVH = 8
HD = 128
M = 16
CODES = 256
BLK = 64
SEL = 16
N = 32
R = 16
T = 256
PAIRS = 4
EARLY = 1
NEGATIVE = -1e30
SCALE = HD ** (-0.5)
F32 = jnp.float32
BF16 = jnp.bfloat16
MESH = pl.DeviceIdType.MESH


def iota(shape, dim):
    return lax.broadcasted_iota(jnp.int32, shape, dim)


def take(table, index):
    return jnp.take_along_axis(table, index, axis=1, mode="promise_in_bounds")


def kernel(
    q_hbm, k_hbm, v_hbm, c_hbm, cb_hbm, len_hbm, blk_hbm,
    att_ref, mass_ref,
    qbuf, qf0, qf1, qp0, qp1, codes, keys, vals, cb, raw_lo, raw_hi, tab_lo, tab_hi,
    khat, lens, blk, chosen, idx_a, idx_b, idx_c, idx_d, guesses, scores, weights, stage, sendbuf, recvbuf, stat, stat_out, stat_in,
    q_own, small_sem, code_sem, key_sem, val_sem,
    q_send, q_recv, o_send, o_recv, s_send, s_recv,
):
    me = lax.axis_index("ctx")

    barrier = pltpu.get_barrier_semaphore()

    def greet(k, carry):
        pl.semaphore_signal(
            barrier, inc=1, device_id={"ctx": lax.rem(me + k, N)}, device_id_type=MESH
        )
        return carry

    lax.fori_loop(1, N, greet, 0)

    own_q = pltpu.make_async_copy(q_hbm, q_own, small_sem.at[0])
    book = pltpu.make_async_copy(cb_hbm, cb, small_sem.at[1])
    lengths = pltpu.make_async_copy(len_hbm, lens, small_sem.at[2])
    selected = pltpu.make_async_copy(blk_hbm, blk, small_sem.at[3])

    def two_codes(n):
        rows = pl.ds(2 * n, 2)
        return pltpu.make_async_copy(c_hbm.at[rows], codes.at[rows], code_sem.at[n])

    all_keys = pltpu.make_async_copy(k_hbm, keys, key_sem)
    all_vals = pltpu.make_async_copy(v_hbm, vals, val_sem)
    book.start()
    two_codes(0).start()
    for copy in (own_q, lengths, selected):
        copy.start()
    for n in range(1, R // 2):
        two_codes(n).start()
    all_keys.start()
    all_vals.start()
    own_q.wait()
    qbuf[me] = q_own[...]

    book.wait()

    def widen(i, carry):
        rows = pl.ds(pl.multiple_of(i * 64, 64), 64)
        wide = cb[rows, :].astype(F32)
        raw_lo[rows, :] = wide[:, :128]
        raw_hi[rows, :] = wide[:, 128:]
        for s in range(8):
            spread = pl.ds(i * 64 + s, 8, stride=8)
            packed = pl.ds(pl.multiple_of(i * 64 + s * 8, 8), 8)
            tab_lo[packed, :] = raw_lo[spread, :]
            tab_hi[packed, :] = raw_hi[spread, :]
        return carry

    lax.fori_loop(0, 16, widen, 0)

    lengths.wait()
    selected.wait()
    names = blk[...].reshape(R * KVH, SEL)
    total = jnp.zeros((R * KVH, T), F32)
    for b in range(T // BLK):
        hit = (names == me * (T // BLK) + b).astype(F32).astype(BF16)
        spot = (iota((SEL, T), 1) // BLK == b).astype(F32).astype(BF16)
        total = total + jnp.dot(hit, spot, preferred_element_type=F32)
    chosen[...] = total

    def decode_row(r, index):
        for i in range(16):
            columns = []
            code = index[i * 8 : i * 8 + 8, :]
            for half in range(2):
                part = code[:, half * 128 : half * 128 + 128]
                low = part & 127
                high = part > 127
                parts = []
                for s in range(8):
                    at = (i * 8 + s) * 8
                    parts.append(
                        jnp.where(
                            high, take(tab_hi[at : at + 8, :], low), take(tab_lo[at : at + 8, :], low)
                        )
                    )
                columns.append(jnp.concatenate(parts, axis=0))
            khat[r, i * 64 : i * 64 + 64, :] = jnp.concatenate(columns, axis=1).astype(BF16)

    two_codes(0).wait()
    two_codes(1).wait()
    idx_a[...] = codes[0].T

    def decode_four(n, carry):
        @pl.when(n < R // 4 - 1)
        def _():
            two_codes(2 * n + 2).wait()
            two_codes(2 * n + 3).wait()

        r = 4 * n
        idx_b[...] = codes[r + 1].T
        decode_row(r, idx_a)
        idx_c[...] = codes[r + 2].T
        decode_row(r + 1, idx_b)
        idx_d[...] = codes[r + 3].T
        decode_row(r + 2, idx_c)
        idx_a[...] = codes[jnp.minimum(r + 4, R - 1)].T
        decode_row(r + 3, idx_d)
        return carry

    lax.fori_loop(0, EARLY, decode_four, 0)
    pl.semaphore_wait(barrier, N - 1)

    def send_query(k, carry):
        pltpu.make_async_remote_copy(
            src_ref=q_own,
            dst_ref=qbuf.at[me],
            send_sem=q_send,
            recv_sem=q_recv,
            device_id={"ctx": lax.rem(me + k, N)},
            device_id_type=MESH,
        ).start()
        return carry

    lax.fori_loop(1, N, send_query, 0)

    lax.fori_loop(EARLY, R // 4, decode_four, 0)

    whole = qbuf.at[pl.ds(0, N - 1)]
    pltpu.make_async_copy(whole, whole, q_recv).wait()
    pltpu.make_async_copy(whole, whole, q_send).wait()
    to_row = iota((HD, HD), 0)
    to_col = iota((HD, HD), 1)
    origin = (to_col & 64) | ((to_col & 7) << 3) | ((to_col >> 3) & 7)
    permute = (to_row == origin).astype(F32).astype(BF16)
    for hh, (plain, turned) in enumerate(((qf0, qp0), (qf1, qp1))):
        part = qbuf[:, :, hh * HD : hh * HD + HD].reshape(N * R, HD)
        plain[...] = part.astype(F32)
        turned[...] = jnp.dot(part, permute, preferred_element_type=F32)

    all_keys.wait()
    all_vals.wait()
    left = (iota((16, 1), 0) & 7) < 4
    left_wide = (iota((16, HD), 0) & 7) < 4
    position = iota((1, T), 1) + me * T
    lane = iota((8, 128), 1)

    def spread_heads(part0, part1, r, p):
        at = pl.ds(p * 128 + r, 8, stride=16)
        both = jnp.concatenate([part0[at, :], part1[at, :]], axis=0)
        return jnp.concatenate(
            [jnp.where(left_wide, both, 0.0), jnp.where(left_wide, 0.0, both)], axis=1
        ).astype(BF16)

    def place(n):
        step = n // 4
        turn = jnp.where(lax.rem(me, 2) == 0, step + 1, 3 - step)
        return lax.rem(me // 8 + turn, PAIRS), lax.rem(n, 4) * 4

    def multiply(n):
        p, first = place(n)
        wide = pl.ds(pl.multiple_of(p * 256, 256), 256)
        for u in range(4):
            r = first + u
            at = slice(u * 16, u * 16 + 16)
            guesses[at, :] = jnp.dot(
                spread_heads(qp0, qp1, r, p), khat[r, wide, :], preferred_element_type=F32
            )
            scores[at, :] = lax.dot_general(
                spread_heads(qf0, qf1, r, p),
                keys[r, :, wide],
                (((1,), (1,)), ((), ())),
                preferred_element_type=F32,
            )

    def weigh(n):
        p, first = place(n)
        eight = pl.ds(pl.multiple_of(p * 8, 8), 8)
        kept = stat[eight, :]
        for u in range(4):
            r = first + u
            at = slice(u * 16, u * 16 + 16)
            inside = position < lens[r]
            guess = jnp.where(inside, guesses[at, :] * SCALE, NEGATIVE)
            guess_peak = jnp.max(guess, axis=1, keepdims=True)
            guess_total = jnp.sum(
                jnp.where(inside, jnp.exp(guess - guess_peak), 0.0), axis=1, keepdims=True
            )
            here = chosen[pl.ds(r * KVH + 2 * p, 1), :]
            there = chosen[pl.ds(r * KVH + 2 * p + 1, 1), :]
            used = (jnp.where(left, here, there) > 0.5) & inside
            score = jnp.where(used, scores[at, :] * SCALE, NEGATIVE)
            peak = jnp.max(score, axis=1, keepdims=True)
            weight = jnp.where(used, jnp.exp(score - peak), 0.0)
            weight_total = jnp.sum(weight, axis=1, keepdims=True)
            weights[at, :] = weight.astype(BF16)
            for kind, value in enumerate((guess_peak, guess_total, peak, weight_total)):
                for hh in range(2):
                    kept = jnp.where(
                        lane == kind * 32 + hh * 16 + r, value[hh * 8 : hh * 8 + 8], kept
                    )
        stat[eight, :] = kept

    def average(n):
        p, first = place(n)
        wide = pl.ds(pl.multiple_of(p * 256, 256), 256)
        for u in range(4):
            r = first + u
            summed = jnp.dot(
                weights[u * 16 : u * 16 + 16, :], vals[r, :, wide], preferred_element_type=F32
            )
            summed = jnp.where(left, summed[:, :HD], summed[:, HD:])
            stage[pl.ds(p * 256 + r, 8, stride=32), :] = summed[:8]
            stage[pl.ds(p * 256 + 16 + r, 8, stride=32), :] = summed[8:]

    def send_stats(n):
        p, _ = place(n)
        for k in range(8):
            stat_out[p * 8 + k] = stat[pl.ds(p * 8 + k, 1), :]

        def send_to(k, inner):
            to = p * 8 + k

            @pl.when(to != me)
            def _():
                pltpu.make_async_remote_copy(
                    src_ref=stat_out.at[to],
                    dst_ref=stat_in.at[me],
                    send_sem=s_send,
                    recv_sem=s_recv,
                    device_id={"ctx": to},
                    device_id_type=MESH,
                ).start()

            return inner

        lax.fori_loop(0, 8, send_to, 0)

    def send_values(n):
        p, _ = place(n)
        block = pl.ds(pl.multiple_of(p * 256, 256), 256)
        sendbuf[block, :] = stage[block, :].astype(BF16)

        def send_to(k, inner):
            to = p * 8 + k

            @pl.when(to != me)
            def _():
                pltpu.make_async_remote_copy(
                    src_ref=sendbuf.at[pl.ds(pl.multiple_of(to * 32, 32), 32)],
                    dst_ref=recvbuf.at[pl.ds(pl.multiple_of(me * 32, 32), 32)],
                    send_sem=o_send,
                    recv_sem=o_recv,
                    device_id={"ctx": to},
                    device_id_type=MESH,
                ).start()

            return inner

        lax.fori_loop(0, 8, send_to, 0)

    multiply(0)
    weigh(0)
    multiply(1)

    def attend(n, carry):
        average(n - 2)
        weigh(n - 1)
        multiply(n)

        @pl.when(lax.rem(n, 4) == 1)
        def _():
            send_stats(n - 2)
            send_values(n - 2)

        return carry

    lax.fori_loop(2, R, attend, 0)
    average(R - 2)
    weigh(R - 1)
    send_stats(R - 1)
    average(R - 1)
    send_values(R - 1)
    mine = pl.ds(pl.multiple_of(me * 32, 32), 32)
    recvbuf[mine, :] = sendbuf[mine, :]
    stat_in[me] = stat_out[me]

    source = iota((N, N * 32), 1) // 32
    spread = (source == iota((N, N * 32), 0)).astype(F32).astype(BF16)
    some = stat_in.at[pl.ds(0, N - 1)]
    pltpu.make_async_copy(some, some, s_recv).wait()
    stats = stat_in[...].reshape(N, 128)
    top = jnp.max(stats, axis=0, keepdims=True)
    factor = jnp.exp(stats - top)
    totals = jnp.sum(factor * pltpu.roll(stats, 96, 1), axis=0, keepdims=True)
    mass = top + jnp.log(totals)
    mass_ref[0:1, :] = mass[:, 0:16]
    mass_ref[1:2, :] = mass[:, 16:32]
    share = (factor / totals)[:, 64:96].T
    mix = jnp.dot(share.astype(BF16), spread, preferred_element_type=F32)
    same = (iota((32, N * 32), 1) & 31) == iota((32, N * 32), 0)
    mix = jnp.where(same, mix, 0.0).astype(BF16)
    some = recvbuf.at[pl.ds(0, (N - 1) * 32)]
    pltpu.make_async_copy(some, some, o_recv).wait()
    result = jnp.dot(mix, recvbuf[...], preferred_element_type=F32)
    att_ref[:, 0:HD] = result[:R].astype(BF16)
    att_ref[:, HD:] = result[R:].astype(BF16)
    some = stat_in.at[pl.ds(0, N - 1)]
    pltpu.make_async_copy(some, some, s_send).wait()
    some = recvbuf.at[pl.ds(0, (N - 1) * 32)]
    pltpu.make_async_copy(some, some, o_send).wait()


def body(queries, keys, values, codes, codebook, lengths, blocks):
    book = codebook.transpose(0, 1, 3, 2).reshape(KVH * M * 8, CODES)
    anywhere = pl.BlockSpec(memory_space=pl.ANY)
    vmem = pl.BlockSpec(memory_space=pltpu.VMEM)
    dma = pltpu.SemaphoreType.DMA
    attended, mass = pl.pallas_call(
        kernel,
        out_shape=(
            pltpu.VMEM((R, 2 * HD), BF16),
            pltpu.VMEM((2, R), F32),
        ),
        in_specs=[anywhere] * 7,
        out_specs=(vmem, vmem),
        scratch_shapes=[
            pltpu.VMEM((N, R, 2 * HD), BF16),
            pltpu.VMEM((N * R, HD), F32),
            pltpu.VMEM((N * R, HD), F32),
            pltpu.VMEM((N * R, HD), F32),
            pltpu.VMEM((N * R, HD), F32),
            pltpu.VMEM((R, T, KVH * M), jnp.int32),
            pltpu.VMEM((R, T, KVH * HD), BF16),
            pltpu.VMEM((R, T, KVH * HD), BF16),
            pltpu.VMEM((KVH * M * 8, CODES), BF16),
            pltpu.VMEM((KVH * M * 8, 128), F32),
            pltpu.VMEM((KVH * M * 8, 128), F32),
            pltpu.VMEM((KVH * M * 8, 128), F32),
            pltpu.VMEM((KVH * M * 8, 128), F32),
            pltpu.VMEM((R, KVH * HD, T), BF16),
            pltpu.SMEM((R,), jnp.int32),
            pltpu.VMEM((R, KVH, SEL), jnp.int32),
            pltpu.VMEM((R * KVH, T), F32),
            pltpu.VMEM((KVH * M, T), jnp.int32),
            pltpu.VMEM((KVH * M, T), jnp.int32),
            pltpu.VMEM((KVH * M, T), jnp.int32),
            pltpu.VMEM((KVH * M, T), jnp.int32),
            pltpu.VMEM((64, T), F32),
            pltpu.VMEM((64, T), F32),
            pltpu.VMEM((64, T), BF16),
            pltpu.VMEM((N * 32, HD), F32),
            pltpu.VMEM((N * 32, HD), BF16),
            pltpu.VMEM((N * 32, HD), BF16),
            pltpu.VMEM((N, 128), F32),
            pltpu.VMEM((N, 1, 128), F32),
            pltpu.VMEM((N, 1, 128), F32),
            pltpu.VMEM((R, 2 * HD), BF16),
            dma((4,)),
            dma((R // 2,)),
            dma, dma,
            dma, dma, dma, dma, dma, dma,
        ],
        compiler_params=pltpu.CompilerParams(
            collective_id=0, has_side_effects=True, vmem_limit_bytes=56 * 2**20
        ),
        name="decode_attention",
    )(queries, keys, values, codes, book, lengths, blocks)

    return attended, mass.T


def solution(mesh):
    placed = (
        P("rows", "ctx"),
        P("rows", "ctx", None),
        P("rows", "ctx", None),
        P("rows", "ctx", None),
        P(),
        P("rows"),
        P("rows", None, None),
    )
    return jax.shard_map(
        body,
        mesh=mesh,
        in_specs=placed,
        out_specs=(P("rows", "ctx"), P("rows", "ctx")),
        check_vma=False,
    )
```

```python
import functools

import jax
import jax.numpy as jnp
from jax import lax
from jax.experimental import pallas as pl
from jax.experimental.pallas import tpu as pltpu
from jax.sharding import PartitionSpec as P

H = 64
KVH = 8
HD = 128
M = 16
CODES = 256
BLK = 64
SEL = 16
N = 32
R = 16
T = 256
PAIRS = 4
EARLY = 1
NEGATIVE = -1e30
SCALE = HD ** (-0.5)
F32 = jnp.float32
BF16 = jnp.bfloat16
MESH = pl.DeviceIdType.MESH


def iota(shape, dim):
    return lax.broadcasted_iota(jnp.int32, shape, dim)


def take(table, index):
    return jnp.take_along_axis(table, index, axis=1, mode="promise_in_bounds")


def kernel(
    q_hbm, k_hbm, v_hbm, c_hbm, cb_hbm, len_hbm, blk_hbm,
    att_ref, mass_ref,
    qbuf, qf0, qf1, qp0, qp1, codes, keys, vals, cb, raw_lo, raw_hi, tab_lo, tab_hi,
    khat, lens, blk, chosen, idx_a, idx_b, idx_c, idx_d, guesses, scores, weights, stage, sendbuf, recvbuf, stat, stat_out, stat_in,
    q_own, small_sem, code_sem, key_sem, val_sem,
    q_send, q_recv, o_send, o_recv, s_send, s_recv,
):
    me = lax.axis_index("ctx")

    barrier = pltpu.get_barrier_semaphore()

    def greet(k, carry):
        pl.semaphore_signal(
            barrier, inc=1, device_id={"ctx": lax.rem(me + k, N)}, device_id_type=MESH
        )
        return carry

    lax.fori_loop(1, N, greet, 0)

    own_q = pltpu.make_async_copy(q_hbm, q_own, small_sem.at[0])
    book = pltpu.make_async_copy(cb_hbm, cb, small_sem.at[1])
    lengths = pltpu.make_async_copy(len_hbm, lens, small_sem.at[2])
    selected = pltpu.make_async_copy(blk_hbm, blk, small_sem.at[3])

    def two_codes(n):
        rows = pl.ds(2 * n, 2)
        return pltpu.make_async_copy(c_hbm.at[rows], codes.at[rows], code_sem.at[n])

    all_keys = pltpu.make_async_copy(k_hbm, keys, key_sem)
    all_vals = pltpu.make_async_copy(v_hbm, vals, val_sem)
    book.start()
    two_codes(0).start()
    for copy in (own_q, lengths, selected):
        copy.start()
    for n in range(1, R // 2):
        two_codes(n).start()
    all_keys.start()
    all_vals.start()
    own_q.wait()
    qbuf[me] = q_own[...]

    book.wait()

    def widen(i, carry):
        rows = pl.ds(pl.multiple_of(i * 64, 64), 64)
        wide = cb[rows, :].astype(F32)
        raw_lo[rows, :] = wide[:, :128]
        raw_hi[rows, :] = wide[:, 128:]
        for s in range(8):
            spread = pl.ds(i * 64 + s, 8, stride=8)
            packed = pl.ds(pl.multiple_of(i * 64 + s * 8, 8), 8)
            tab_lo[packed, :] = raw_lo[spread, :]
            tab_hi[packed, :] = raw_hi[spread, :]
        return carry

    lax.fori_loop(0, 16, widen, 0)

    def decode_row(r, index):
        for i in range(16):
            columns = []
            code = index[i * 8 : i * 8 + 8, :]
            for half in range(2):
                part = code[:, half * 128 : half * 128 + 128]
                low = part & 127
                high = part > 127
                parts = []
                for s in range(8):
                    at = (i * 8 + s) * 8
                    parts.append(
                        jnp.where(
                            high, take(tab_hi[at : at + 8, :], low), take(tab_lo[at : at + 8, :], low)
                        )
                    )
                columns.append(jnp.concatenate(parts, axis=0))
            khat[r, i * 64 : i * 64 + 64, :] = jnp.concatenate(columns, axis=1).astype(BF16)

    two_codes(0).wait()
    two_codes(1).wait()
    idx_a[...] = codes[0].T

    def decode_four(n, carry):
        @pl.when(n < R // 4 - 1)
        def _():
            two_codes(2 * n + 2).wait()
            two_codes(2 * n + 3).wait()

        r = 4 * n
        idx_b[...] = codes[r + 1].T
        decode_row(r, idx_a)
        idx_c[...] = codes[r + 2].T
        decode_row(r + 1, idx_b)
        idx_d[...] = codes[r + 3].T
        decode_row(r + 2, idx_c)
        idx_a[...] = codes[jnp.minimum(r + 4, R - 1)].T
        decode_row(r + 3, idx_d)
        return carry

    lax.fori_loop(0, EARLY, decode_four, 0)
    pl.semaphore_wait(barrier, N - 1)

    def send_query(k, carry):
        pltpu.make_async_remote_copy(
            src_ref=q_own,
            dst_ref=qbuf.at[me],
            send_sem=q_send,
            recv_sem=q_recv,
            device_id={"ctx": lax.rem(me + k, N)},
            device_id_type=MESH,
        ).start()
        return carry

    lax.fori_loop(1, N, send_query, 0)

    lengths.wait()
    selected.wait()
    names = blk[...].reshape(R * KVH, SEL)
    total = jnp.zeros((R * KVH, T), F32)
    for b in range(T // BLK):
        hit = (names == me * (T // BLK) + b).astype(F32).astype(BF16)
        spot = (iota((SEL, T), 1) // BLK == b).astype(F32).astype(BF16)
        total = total + jnp.dot(hit, spot, preferred_element_type=F32)
    chosen[...] = total


    lax.fori_loop(EARLY, R // 4, decode_four, 0)

    whole = qbuf.at[pl.ds(0, N - 1)]
    pltpu.make_async_copy(whole, whole, q_recv).wait()
    pltpu.make_async_copy(whole, whole, q_send).wait()
    to_row = iota((HD, HD), 0)
    to_col = iota((HD, HD), 1)
    origin = (to_col & 64) | ((to_col & 7) << 3) | ((to_col >> 3) & 7)
    permute = (to_row == origin).astype(F32).astype(BF16)
    for hh, (plain, turned) in enumerate(((qf0, qp0), (qf1, qp1))):
        part = qbuf[:, :, hh * HD : hh * HD + HD].reshape(N * R, HD)
        plain[: N * R, :] = part.astype(F32)
        turned[: N * R, :] = jnp.dot(part, permute, preferred_element_type=F32)

    all_keys.wait()
    all_vals.wait()
    left = (iota((16, 1), 0) & 7) < 4
    left_wide = (iota((16, HD), 0) & 7) < 4
    position = iota((1, T), 1) + me * T
    lane = iota((8, 128), 1)

    def spread_heads(part0, part1, r, p):
        at = pl.ds(p * 128 + r, 8, stride=16)
        both = jnp.concatenate([part0[at, :], part1[at, :]], axis=0)
        return jnp.concatenate(
            [jnp.where(left_wide, both, 0.0), jnp.where(left_wide, 0.0, both)], axis=1
        ).astype(BF16)

    def place(n):
        step = n // 4
        turn = jnp.where(lax.rem(me, 2) == 0, step + 1, 3 - step)
        return lax.rem(me // 8 + turn, PAIRS), lax.rem(n, 4) * 4

    def multiply(n):
        p, first = place(n)
        wide = pl.ds(pl.multiple_of(p * 256, 256), 256)
        for u in range(4):
            r = first + u
            at = slice(u * 16, u * 16 + 16)
            guesses[at, :] = jnp.dot(
                spread_heads(qp0, qp1, r, p), khat[r, wide, :], preferred_element_type=F32
            )
            scores[at, :] = lax.dot_general(
                spread_heads(qf0, qf1, r, p),
                keys[r, :, wide],
                (((1,), (1,)), ((), ())),
                preferred_element_type=F32,
            )

    def weigh(n):
        p, first = place(n)
        eight = pl.ds(pl.multiple_of(p * 8, 8), 8)
        kept = stat[eight, :]
        for u in range(4):
            r = first + u
            at = slice(u * 16, u * 16 + 16)
            inside = position < lens[r]
            guess = jnp.where(inside, guesses[at, :] * SCALE, NEGATIVE)
            guess_peak = jnp.max(guess, axis=1, keepdims=True)
            guess_total = jnp.sum(
                jnp.where(inside, jnp.exp(guess - guess_peak), 0.0), axis=1, keepdims=True
            )
            here = chosen[pl.ds(r * KVH + 2 * p, 1), :]
            there = chosen[pl.ds(r * KVH + 2 * p + 1, 1), :]
            used = (jnp.where(left, here, there) > 0.5) & inside
            score = jnp.where(used, scores[at, :] * SCALE, NEGATIVE)
            peak = jnp.max(score, axis=1, keepdims=True)
            weight = jnp.where(used, jnp.exp(score - peak), 0.0)
            weight_total = jnp.sum(weight, axis=1, keepdims=True)
            weights[at, :] = weight.astype(BF16)
            for kind, value in enumerate((guess_peak, guess_total, peak, weight_total)):
                for hh in range(2):
                    kept = jnp.where(
                        lane == kind * 32 + hh * 16 + r, value[hh * 8 : hh * 8 + 8], kept
                    )
        stat[eight, :] = kept

    def average(n):
        p, first = place(n)
        wide = pl.ds(pl.multiple_of(p * 256, 256), 256)
        for u in range(4):
            r = first + u
            summed = jnp.dot(
                weights[u * 16 : u * 16 + 16, :], vals[r, :, wide], preferred_element_type=F32
            )
            summed = jnp.where(left, summed[:, :HD], summed[:, HD:])
            stage[pl.ds(p * 256 + r, 8, stride=32), :] = summed[:8]
            stage[pl.ds(p * 256 + 16 + r, 8, stride=32), :] = summed[8:]

    def send_stats(n):
        p, _ = place(n)
        for k in range(8):
            stat_out[p * 8 + k] = stat[pl.ds(p * 8 + k, 1), :]

        def send_to(k, inner):
            to = p * 8 + lax.rem(me + 4 + k, 8)

            @pl.when(to != me)
            def _():
                pltpu.make_async_remote_copy(
                    src_ref=stat_out.at[to],
                    dst_ref=stat_in.at[me],
                    send_sem=s_send,
                    recv_sem=s_recv,
                    device_id={"ctx": to},
                    device_id_type=MESH,
                ).start()

            return inner

        lax.fori_loop(0, 8, send_to, 0)

    def send_values(n):
        p, _ = place(n)
        block = pl.ds(pl.multiple_of(p * 256, 256), 256)
        sendbuf[block, :] = stage[block, :].astype(BF16)

        def send_to(k, inner):
            to = p * 8 + lax.rem(me + 4 + k, 8)

            @pl.when(to != me)
            def _():
                pltpu.make_async_remote_copy(
                    src_ref=sendbuf.at[pl.ds(pl.multiple_of(to * 32, 32), 32)],
                    dst_ref=recvbuf.at[pl.ds(pl.multiple_of(me * 32, 32), 32)],
                    send_sem=o_send,
                    recv_sem=o_recv,
                    device_id={"ctx": to},
                    device_id_type=MESH,
                ).start()

            return inner

        lax.fori_loop(0, 8, send_to, 0)

    multiply(0)
    weigh(0)
    multiply(1)

    def attend(n, carry):
        average(n - 2)
        weigh(n - 1)
        multiply(n)

        @pl.when(lax.rem(n, 4) == 1)
        def _():
            send_stats(n - 2)
            send_values(n - 2)

        return carry

    lax.fori_loop(2, R, attend, 0)
    average(R - 2)
    weigh(R - 1)
    send_stats(R - 1)
    average(R - 1)
    send_values(R - 1)
    mine = pl.ds(pl.multiple_of(me * 32, 32), 32)
    recvbuf[mine, :] = sendbuf[mine, :]
    stat_in[me] = stat_out[me]

    source = iota((N, N * 32), 1) // 32
    spread = (source == iota((N, N * 32), 0)).astype(F32).astype(BF16)
    some = stat_in.at[pl.ds(0, N - 1)]
    pltpu.make_async_copy(some, some, s_recv).wait()
    stats = stat_in[...].reshape(N, 128)
    top = jnp.max(stats, axis=0, keepdims=True)
    factor = jnp.exp(stats - top)
    totals = jnp.sum(factor * pltpu.roll(stats, 96, 1), axis=0, keepdims=True)
    mass = top + jnp.log(totals)
    mass_ref[0:1, :] = mass[:, 0:16]
    mass_ref[1:2, :] = mass[:, 16:32]
    share = (factor / totals)[:, 64:96].T
    mix = jnp.dot(share.astype(BF16), spread, preferred_element_type=F32)
    same = (iota((32, N * 32), 1) & 31) == iota((32, N * 32), 0)
    mix = jnp.where(same, mix, 0.0).astype(BF16)
    some = recvbuf.at[pl.ds(0, (N - 1) * 32)]
    pltpu.make_async_copy(some, some, o_recv).wait()
    result = jnp.dot(mix, recvbuf[...], preferred_element_type=F32)
    att_ref[:, 0:HD] = result[:R].astype(BF16)
    att_ref[:, HD:] = result[R:].astype(BF16)
    some = stat_in.at[pl.ds(0, N - 1)]
    pltpu.make_async_copy(some, some, s_send).wait()
    some = recvbuf.at[pl.ds(0, (N - 1) * 32)]
    pltpu.make_async_copy(some, some, o_send).wait()


def body(queries, keys, values, codes, codebook, lengths, blocks):
    book = codebook.transpose(0, 1, 3, 2).reshape(KVH * M * 8, CODES)
    anywhere = pl.BlockSpec(memory_space=pl.ANY)
    vmem = pl.BlockSpec(memory_space=pltpu.VMEM)
    dma = pltpu.SemaphoreType.DMA
    attended, mass = pl.pallas_call(
        kernel,
        out_shape=(
            pltpu.VMEM((R, 2 * HD), BF16),
            pltpu.VMEM((2, R), F32),
        ),
        in_specs=[anywhere] * 7,
        out_specs=(vmem, vmem),
        scratch_shapes=[
            pltpu.VMEM((N, R, 2 * HD), BF16),
            pltpu.VMEM((N * R + 16, HD), F32),
            pltpu.VMEM((N * R + 16, HD), F32),
            pltpu.VMEM((N * R + 16, HD), F32),
            pltpu.VMEM((N * R + 16, HD), F32),
            pltpu.VMEM((R, T, KVH * M), jnp.int32),
            pltpu.VMEM((R, T, KVH * HD), BF16),
            pltpu.VMEM((R, T, KVH * HD), BF16),
            pltpu.VMEM((KVH * M * 8, CODES), BF16),
            pltpu.VMEM((KVH * M * 8 + 64, 128), F32),
            pltpu.VMEM((KVH * M * 8 + 64, 128), F32),
            pltpu.VMEM((KVH * M * 8, 128), F32),
            pltpu.VMEM((KVH * M * 8, 128), F32),
            pltpu.VMEM((R, KVH * HD, T), BF16),
            pltpu.SMEM((R,), jnp.int32),
            pltpu.VMEM((R, KVH, SEL), jnp.int32),
            pltpu.VMEM((R * KVH, T), F32),
            pltpu.VMEM((KVH * M, T), jnp.int32),
            pltpu.VMEM((KVH * M, T), jnp.int32),
            pltpu.VMEM((KVH * M, T), jnp.int32),
            pltpu.VMEM((KVH * M, T), jnp.int32),
            pltpu.VMEM((64, T), F32),
            pltpu.VMEM((64, T), F32),
            pltpu.VMEM((64, T), BF16),
            pltpu.VMEM((N * 32 + 32, HD), F32),
            pltpu.VMEM((N * 32, HD), BF16),
            pltpu.VMEM((N * 32, HD), BF16),
            pltpu.VMEM((N, 128), F32),
            pltpu.VMEM((N, 1, 128), F32),
            pltpu.VMEM((N, 1, 128), F32),
            pltpu.VMEM((R, 2 * HD), BF16),
            dma((4,)),
            dma((R // 2,)),
            dma, dma,
            dma, dma, dma, dma, dma, dma,
        ],
        compiler_params=pltpu.CompilerParams(
            collective_id=0, has_side_effects=True, vmem_limit_bytes=56 * 2**20
        ),
        name="decode_attention",
    )(queries, keys, values, codes, book, lengths, blocks)

    return attended, mass.T


def solution(mesh):
    placed = (
        P("rows", "ctx"),
        P("rows", "ctx", None),
        P("rows", "ctx", None),
        P("rows", "ctx", None),
        P(),
        P("rows"),
        P("rows", None, None),
    )
    return jax.shard_map(
        body,
        mesh=mesh,
        in_specs=placed,
        out_specs=(P("rows", "ctx"), P("rows", "ctx")),
        check_vma=False,
    )
```

```python
import functools

import jax
import jax.numpy as jnp
from jax import lax
from jax.experimental import pallas as pl
from jax.experimental.pallas import tpu as pltpu
from jax.sharding import PartitionSpec as P

H = 64
KVH = 8
HD = 128
M = 16
CODES = 256
BLK = 64
SEL = 16
N = 32
R = 16
T = 256
PAIRS = 4
EARLY = 1
NEGATIVE = -1e30
SCALE = HD ** (-0.5)
F32 = jnp.float32
BF16 = jnp.bfloat16
MESH = pl.DeviceIdType.MESH


def iota(shape, dim):
    return lax.broadcasted_iota(jnp.int32, shape, dim)


def take(table, index):
    return jnp.take_along_axis(table, index, axis=1, mode="promise_in_bounds")


def kernel(
    q_hbm, k_hbm, v_hbm, c_hbm, cb_hbm, len_hbm, blk_hbm,
    att_ref, mass_ref,
    qbuf, qf0, qf1, qp0, qp1, codes, keys, vals, cb, raw_lo, raw_hi, tab_lo, tab_hi,
    khat, lens, blk, chosen, idx_a, idx_b, idx_c, idx_d, guesses, scores, weights, stage, sendbuf, recvbuf, stat, stat_out, stat_in,
    q_own, small_sem, code_sem, key_sem, val_sem,
    q_send, q_recv, o_send, o_recv, s_send, s_recv,
):
    me = lax.axis_index("ctx")

    barrier = pltpu.get_barrier_semaphore()

    def greet(k, carry):
        pl.semaphore_signal(
            barrier, inc=1, device_id={"ctx": lax.rem(me + k, N)}, device_id_type=MESH
        )
        return carry

    lax.fori_loop(1, N, greet, 0)

    own_q = pltpu.make_async_copy(q_hbm, q_own, small_sem.at[0])
    book = pltpu.make_async_copy(cb_hbm, cb, small_sem.at[1])
    lengths = pltpu.make_async_copy(len_hbm, lens, small_sem.at[2])
    selected = pltpu.make_async_copy(blk_hbm, blk, small_sem.at[3])

    def two_codes(n):
        rows = pl.ds(2 * n, 2)
        return pltpu.make_async_copy(c_hbm.at[rows], codes.at[rows], code_sem.at[n])

    all_keys = pltpu.make_async_copy(k_hbm, keys, key_sem)
    all_vals = pltpu.make_async_copy(v_hbm, vals, val_sem)
    book.start()
    two_codes(0).start()
    for copy in (own_q, lengths, selected):
        copy.start()
    for n in range(1, R // 2):
        two_codes(n).start()
    all_keys.start()
    all_vals.start()
    own_q.wait()
    qbuf[me] = q_own[...]

    book.wait()

    def widen(i, carry):
        rows = pl.ds(pl.multiple_of(i * 64, 64), 64)
        wide = cb[rows, :].astype(F32)
        raw_lo[rows, :] = wide[:, :128]
        raw_hi[rows, :] = wide[:, 128:]
        for s in range(8):
            spread = pl.ds(i * 64 + s, 8, stride=8)
            packed = pl.ds(pl.multiple_of(i * 64 + s * 8, 8), 8)
            tab_lo[packed, :] = raw_lo[spread, :]
            tab_hi[packed, :] = raw_hi[spread, :]
        return carry

    lax.fori_loop(0, 16, widen, 0)

    unit = (iota((128, 128), 0) == iota((128, 128), 1)).astype(F32).astype(BF16)

    def flipped(r):
        flat = codes[r].astype(F32).astype(BF16)
        return lax.dot_general(
            unit, flat, (((1,), (1,)), ((), ())), preferred_element_type=F32
        ).astype(jnp.int32)

    def decode_row(r, index):
        for i in range(16):
            columns = []
            code = index[i * 8 : i * 8 + 8, :]
            for half in range(2):
                part = code[:, half * 128 : half * 128 + 128]
                low = part & 127
                high = part > 127
                parts = []
                for s in range(8):
                    at = (i * 8 + s) * 8
                    parts.append(
                        jnp.where(
                            high, take(tab_hi[at : at + 8, :], low), take(tab_lo[at : at + 8, :], low)
                        )
                    )
                columns.append(jnp.concatenate(parts, axis=0))
            khat[r, i * 64 : i * 64 + 64, :] = jnp.concatenate(columns, axis=1).astype(BF16)

    two_codes(0).wait()
    two_codes(1).wait()
    idx_a[...] = flipped(0)

    def decode_four(n, carry):
        @pl.when(n < R // 4 - 1)
        def _():
            two_codes(2 * n + 2).wait()
            two_codes(2 * n + 3).wait()

        r = 4 * n
        idx_b[...] = flipped(r + 1)
        decode_row(r, idx_a)
        idx_c[...] = flipped(r + 2)
        decode_row(r + 1, idx_b)
        idx_d[...] = flipped(r + 3)
        decode_row(r + 2, idx_c)
        idx_a[...] = flipped(jnp.minimum(r + 4, R - 1))
        decode_row(r + 3, idx_d)
        return carry

    lax.fori_loop(0, EARLY, decode_four, 0)
    pl.semaphore_wait(barrier, N - 1)

    def send_query(k, carry):
        pltpu.make_async_remote_copy(
            src_ref=q_own,
            dst_ref=qbuf.at[me],
            send_sem=q_send,
            recv_sem=q_recv,
            device_id={"ctx": lax.rem(me + k, N)},
            device_id_type=MESH,
        ).start()
        return carry

    lax.fori_loop(1, N, send_query, 0)

    lengths.wait()
    selected.wait()
    names = blk[...].reshape(R * KVH, SEL)
    total = jnp.zeros((R * KVH, T), F32)
    for b in range(T // BLK):
        hit = (names == me * (T // BLK) + b).astype(F32).astype(BF16)
        spot = (iota((SEL, T), 1) // BLK == b).astype(F32).astype(BF16)
        total = total + jnp.dot(hit, spot, preferred_element_type=F32)
    chosen[...] = total


    lax.fori_loop(EARLY, R // 4, decode_four, 0)

    whole = qbuf.at[pl.ds(0, N - 1)]
    pltpu.make_async_copy(whole, whole, q_recv).wait()
    pltpu.make_async_copy(whole, whole, q_send).wait()
    to_row = iota((HD, HD), 0)
    to_col = iota((HD, HD), 1)
    origin = (to_col & 64) | ((to_col & 7) << 3) | ((to_col >> 3) & 7)
    permute = (to_row == origin).astype(F32).astype(BF16)
    for hh, (plain, turned) in enumerate(((qf0, qp0), (qf1, qp1))):
        part = qbuf[:, :, hh * HD : hh * HD + HD].reshape(N * R, HD)
        plain[: N * R, :] = part.astype(F32)
        turned[: N * R, :] = jnp.dot(part, permute, preferred_element_type=F32)

    all_keys.wait()
    all_vals.wait()
    left = (iota((16, 1), 0) & 7) < 4
    left_wide = (iota((16, HD), 0) & 7) < 4
    position = iota((1, T), 1) + me * T
    lane = iota((8, 128), 1)

    def spread_heads(part0, part1, r, p):
        at = pl.ds(p * 128 + r, 8, stride=16)
        both = jnp.concatenate([part0[at, :], part1[at, :]], axis=0)
        return jnp.concatenate(
            [jnp.where(left_wide, both, 0.0), jnp.where(left_wide, 0.0, both)], axis=1
        ).astype(BF16)

    def place(n):
        step = n // 4
        turn = jnp.where(lax.rem(me, 2) == 0, step + 1, 3 - step)
        return lax.rem(me // 8 + turn, PAIRS), lax.rem(n, 4) * 4

    def multiply(n):
        p, first = place(n)
        wide = pl.ds(pl.multiple_of(p * 256, 256), 256)
        for u in range(4):
            r = first + u
            at = slice(u * 16, u * 16 + 16)
            guesses[at, :] = jnp.dot(
                spread_heads(qp0, qp1, r, p), khat[r, wide, :], preferred_element_type=F32
            )
            scores[at, :] = lax.dot_general(
                spread_heads(qf0, qf1, r, p),
                keys[r, :, wide],
                (((1,), (1,)), ((), ())),
                preferred_element_type=F32,
            )

    def weigh(n):
        p, first = place(n)
        eight = pl.ds(pl.multiple_of(p * 8, 8), 8)
        kept = stat[eight, :]
        for u in range(4):
            r = first + u
            at = slice(u * 16, u * 16 + 16)
            inside = position < lens[r]
            guess = jnp.where(inside, guesses[at, :] * SCALE, NEGATIVE)
            guess_peak = jnp.max(guess, axis=1, keepdims=True)
            guess_total = jnp.sum(
                jnp.where(inside, jnp.exp(guess - guess_peak), 0.0), axis=1, keepdims=True
            )
            here = chosen[pl.ds(r * KVH + 2 * p, 1), :]
            there = chosen[pl.ds(r * KVH + 2 * p + 1, 1), :]
            used = (jnp.where(left, here, there) > 0.5) & inside
            score = jnp.where(used, scores[at, :] * SCALE, NEGATIVE)
            peak = jnp.max(score, axis=1, keepdims=True)
            weight = jnp.where(used, jnp.exp(score - peak), 0.0)
            weight_total = jnp.sum(weight, axis=1, keepdims=True)
            weights[at, :] = weight.astype(BF16)
            for kind, value in enumerate((guess_peak, guess_total, peak, weight_total)):
                for hh in range(2):
                    kept = jnp.where(
                        lane == kind * 32 + hh * 16 + r, value[hh * 8 : hh * 8 + 8], kept
                    )
        stat[eight, :] = kept

    def average(n):
        p, first = place(n)
        wide = pl.ds(pl.multiple_of(p * 256, 256), 256)
        for u in range(4):
            r = first + u
            summed = jnp.dot(
                weights[u * 16 : u * 16 + 16, :], vals[r, :, wide], preferred_element_type=F32
            )
            summed = jnp.where(left, summed[:, :HD], summed[:, HD:])
            stage[pl.ds(p * 256 + r, 8, stride=32), :] = summed[:8]
            stage[pl.ds(p * 256 + 16 + r, 8, stride=32), :] = summed[8:]

    def send_stats(n):
        p, _ = place(n)
        for k in range(8):
            stat_out[p * 8 + k] = stat[pl.ds(p * 8 + k, 1), :]

        def send_to(k, inner):
            to = p * 8 + lax.rem(me + 4 + k, 8)

            @pl.when(to != me)
            def _():
                pltpu.make_async_remote_copy(
                    src_ref=stat_out.at[to],
                    dst_ref=stat_in.at[me],
                    send_sem=s_send,
                    recv_sem=s_recv,
                    device_id={"ctx": to},
                    device_id_type=MESH,
                ).start()

            return inner

        lax.fori_loop(0, 8, send_to, 0)

    def send_values(n):
        p, _ = place(n)
        block = pl.ds(pl.multiple_of(p * 256, 256), 256)
        sendbuf[block, :] = stage[block, :].astype(BF16)

        def send_to(k, inner):
            to = p * 8 + lax.rem(me + 4 + k, 8)

            @pl.when(to != me)
            def _():
                pltpu.make_async_remote_copy(
                    src_ref=sendbuf.at[pl.ds(pl.multiple_of(to * 32, 32), 32)],
                    dst_ref=recvbuf.at[pl.ds(pl.multiple_of(me * 32, 32), 32)],
                    send_sem=o_send,
                    recv_sem=o_recv,
                    device_id={"ctx": to},
                    device_id_type=MESH,
                ).start()

            return inner

        lax.fori_loop(0, 8, send_to, 0)

    multiply(0)
    weigh(0)
    multiply(1)

    def attend(n, carry):
        average(n - 2)
        weigh(n - 1)
        multiply(n)

        @pl.when(lax.rem(n, 4) == 1)
        def _():
            send_stats(n - 2)
            send_values(n - 2)

        return carry

    lax.fori_loop(2, R, attend, 0)
    average(R - 2)
    weigh(R - 1)
    send_stats(R - 1)
    average(R - 1)
    send_values(R - 1)
    mine = pl.ds(pl.multiple_of(me * 32, 32), 32)
    recvbuf[mine, :] = sendbuf[mine, :]
    stat_in[me] = stat_out[me]

    source = iota((N, N * 32), 1) // 32
    spread = (source == iota((N, N * 32), 0)).astype(F32).astype(BF16)
    some = stat_in.at[pl.ds(0, N - 1)]
    pltpu.make_async_copy(some, some, s_recv).wait()
    stats = stat_in[...].reshape(N, 128)
    top = jnp.max(stats, axis=0, keepdims=True)
    factor = jnp.exp(stats - top)
    totals = jnp.sum(factor * pltpu.roll(stats, 96, 1), axis=0, keepdims=True)
    mass = top + jnp.log(totals)
    mass_ref[0:1, :] = mass[:, 0:16]
    mass_ref[1:2, :] = mass[:, 16:32]
    share = (factor / totals)[:, 64:96].T
    mix = jnp.dot(share.astype(BF16), spread, preferred_element_type=F32)
    same = (iota((32, N * 32), 1) & 31) == iota((32, N * 32), 0)
    mix = jnp.where(same, mix, 0.0).astype(BF16)
    some = recvbuf.at[pl.ds(0, (N - 1) * 32)]
    pltpu.make_async_copy(some, some, o_recv).wait()
    result = jnp.dot(mix, recvbuf[...], preferred_element_type=F32)
    att_ref[:, 0:HD] = result[:R].astype(BF16)
    att_ref[:, HD:] = result[R:].astype(BF16)
    some = stat_in.at[pl.ds(0, N - 1)]
    pltpu.make_async_copy(some, some, s_send).wait()
    some = recvbuf.at[pl.ds(0, (N - 1) * 32)]
    pltpu.make_async_copy(some, some, o_send).wait()


def body(queries, keys, values, codes, codebook, lengths, blocks):
    book = codebook.transpose(0, 1, 3, 2).reshape(KVH * M * 8, CODES)
    anywhere = pl.BlockSpec(memory_space=pl.ANY)
    vmem = pl.BlockSpec(memory_space=pltpu.VMEM)
    dma = pltpu.SemaphoreType.DMA
    attended, mass = pl.pallas_call(
        kernel,
        out_shape=(
            pltpu.VMEM((R, 2 * HD), BF16),
            pltpu.VMEM((2, R), F32),
        ),
        in_specs=[anywhere] * 7,
        out_specs=(vmem, vmem),
        scratch_shapes=[
            pltpu.VMEM((N, R, 2 * HD), BF16),
            pltpu.VMEM((N * R + 16, HD), F32),
            pltpu.VMEM((N * R + 16, HD), F32),
            pltpu.VMEM((N * R + 16, HD), F32),
            pltpu.VMEM((N * R + 16, HD), F32),
            pltpu.VMEM((R, T, KVH * M), jnp.int32),
            pltpu.VMEM((R, T, KVH * HD), BF16),
            pltpu.VMEM((R, T, KVH * HD), BF16),
            pltpu.VMEM((KVH * M * 8, CODES), BF16),
            pltpu.VMEM((KVH * M * 8 + 64, 128), F32),
            pltpu.VMEM((KVH * M * 8 + 64, 128), F32),
            pltpu.VMEM((KVH * M * 8, 128), F32),
            pltpu.VMEM((KVH * M * 8, 128), F32),
            pltpu.VMEM((R, KVH * HD, T), BF16),
            pltpu.SMEM((R,), jnp.int32),
            pltpu.VMEM((R, KVH, SEL), jnp.int32),
            pltpu.VMEM((R * KVH, T), F32),
            pltpu.VMEM((KVH * M, T), jnp.int32),
            pltpu.VMEM((KVH * M, T), jnp.int32),
            pltpu.VMEM((KVH * M, T), jnp.int32),
            pltpu.VMEM((KVH * M, T), jnp.int32),
            pltpu.VMEM((64, T), F32),
            pltpu.VMEM((64, T), F32),
            pltpu.VMEM((64, T), BF16),
            pltpu.VMEM((N * 32 + 32, HD), F32),
            pltpu.VMEM((N * 32, HD), BF16),
            pltpu.VMEM((N * 32, HD), BF16),
            pltpu.VMEM((N, 128), F32),
            pltpu.VMEM((N, 1, 128), F32),
            pltpu.VMEM((N, 1, 128), F32),
            pltpu.VMEM((R, 2 * HD), BF16),
            dma((4,)),
            dma((R // 2,)),
            dma, dma,
            dma, dma, dma, dma, dma, dma,
        ],
        compiler_params=pltpu.CompilerParams(
            collective_id=0, has_side_effects=True, vmem_limit_bytes=56 * 2**20
        ),
        name="decode_attention",
    )(queries, keys, values, codes, book, lengths, blocks)

    return attended, mass.T


def solution(mesh):
    placed = (
        P("rows", "ctx"),
        P("rows", "ctx", None),
        P("rows", "ctx", None),
        P("rows", "ctx", None),
        P(),
        P("rows"),
        P("rows", None, None),
    )
    return jax.shard_map(
        body,
        mesh=mesh,
        in_specs=placed,
        out_specs=(P("rows", "ctx"), P("rows", "ctx")),
        check_vma=False,
    )
```

```python
import functools

import jax
import jax.numpy as jnp
from jax import lax
from jax.experimental import pallas as pl
from jax.experimental.pallas import tpu as pltpu
from jax.sharding import PartitionSpec as P

H = 64
KVH = 8
HD = 128
M = 16
CODES = 256
BLK = 64
SEL = 16
N = 32
R = 16
T = 256
PAIRS = 4
EARLY = 1
NEGATIVE = -1e30
SCALE = HD ** (-0.5)
F32 = jnp.float32
BF16 = jnp.bfloat16
MESH = pl.DeviceIdType.MESH


def iota(shape, dim):
    return lax.broadcasted_iota(jnp.int32, shape, dim)


def take(table, index):
    return jnp.take_along_axis(table, index, axis=1, mode="promise_in_bounds")


def kernel(
    q_hbm, k_hbm, v_hbm, c_hbm, cb_hbm, len_hbm, blk_hbm,
    att_ref, mass_ref,
    qbuf, qf0, qf1, qp0, qp1, codes, keys, vals, cb, raw_lo, raw_hi, tab_lo, tab_hi,
    khat, lens, blk, chosen, idx_a, idx_b, idx_c, idx_d, guesses, scores, weights, stage, sendbuf, recvbuf, stat, stat_out, stat_in,
    q_own, small_sem, code_sem, key_sem, val_sem,
    q_send, q_recv, o_send, o_recv, s_send, s_recv,
):
    me = lax.axis_index("ctx")

    barrier = pltpu.get_barrier_semaphore()

    def greet(k, carry):
        pl.semaphore_signal(
            barrier, inc=1, device_id={"ctx": lax.rem(me + k, N)}, device_id_type=MESH
        )
        return carry

    lax.fori_loop(1, N, greet, 0)

    own_q = pltpu.make_async_copy(q_hbm, q_own, small_sem.at[0])
    book = pltpu.make_async_copy(cb_hbm, cb, small_sem.at[1])
    lengths = pltpu.make_async_copy(len_hbm, lens, small_sem.at[2])
    selected = pltpu.make_async_copy(blk_hbm, blk, small_sem.at[3])

    def two_codes(n):
        rows = pl.ds(2 * n, 2)
        return pltpu.make_async_copy(c_hbm.at[rows], codes.at[rows], code_sem.at[n])

    all_keys = pltpu.make_async_copy(k_hbm, keys, key_sem)
    all_vals = pltpu.make_async_copy(v_hbm, vals, val_sem)
    book.start()
    two_codes(0).start()
    for copy in (own_q, lengths, selected):
        copy.start()
    for n in range(1, R // 2):
        two_codes(n).start()
    all_keys.start()
    all_vals.start()
    own_q.wait()
    qbuf[me] = q_own[...]

    book.wait()

    def widen(i, carry):
        rows = pl.ds(pl.multiple_of(i * 64, 64), 64)
        wide = cb[rows, :].astype(F32)
        raw_lo[rows, :] = wide[:, :128]
        raw_hi[rows, :] = wide[:, 128:]
        for s in range(8):
            spread = pl.ds(i * 64 + s, 8, stride=8)
            packed = pl.ds(pl.multiple_of(i * 64 + s * 8, 8), 8)
            tab_lo[packed, :] = raw_lo[spread, :]
            tab_hi[packed, :] = raw_hi[spread, :]
        return carry

    lax.fori_loop(0, 16, widen, 0)

    unit = (iota((128, 128), 0) == iota((128, 128), 1)).astype(F32).astype(BF16)

    def flipped(r):
        flat = codes[r].astype(F32).astype(BF16)
        return lax.dot_general(
            unit, flat, (((1,), (1,)), ((), ())), preferred_element_type=F32
        ).astype(jnp.int32)

    def decode_row(r, index):
        for i in range(16):
            columns = []
            code = index[i * 8 : i * 8 + 8, :]
            for half in range(2):
                part = code[:, half * 128 : half * 128 + 128]
                low = part & 127
                high = part > 127
                parts = []
                for s in range(8):
                    at = (i * 8 + s) * 8
                    parts.append(
                        jnp.where(
                            high, take(tab_hi[at : at + 8, :], low), take(tab_lo[at : at + 8, :], low)
                        )
                    )
                columns.append(jnp.concatenate(parts, axis=0))
            khat[r, i * 64 : i * 64 + 64, :] = jnp.concatenate(columns, axis=1).astype(BF16)

    two_codes(0).wait()
    two_codes(1).wait()
    idx_a[...] = flipped(0)

    def decode_four(n, carry):
        @pl.when(n < R // 4 - 1)
        def _():
            two_codes(2 * n + 2).wait()
            two_codes(2 * n + 3).wait()

        r = 4 * n
        idx_b[...] = flipped(r + 1)
        decode_row(r, idx_a)
        idx_c[...] = flipped(r + 2)
        decode_row(r + 1, idx_b)
        idx_d[...] = flipped(r + 3)
        decode_row(r + 2, idx_c)
        idx_a[...] = flipped(jnp.minimum(r + 4, R - 1))
        decode_row(r + 3, idx_d)
        return carry

    lax.fori_loop(0, EARLY, decode_four, 0)
    pl.semaphore_wait(barrier, N - 1)

    def send_query(k, carry):
        pltpu.make_async_remote_copy(
            src_ref=q_own,
            dst_ref=qbuf.at[me],
            send_sem=q_send,
            recv_sem=q_recv,
            device_id={"ctx": lax.rem(me + k, N)},
            device_id_type=MESH,
        ).start()
        return carry

    lax.fori_loop(1, N, send_query, 0)

    lengths.wait()
    selected.wait()
    names = blk[...].reshape(R * KVH, SEL)
    total = jnp.zeros((R * KVH, T), F32)
    for b in range(T // BLK):
        hit = (names == me * (T // BLK) + b).astype(F32).astype(BF16)
        spot = (iota((SEL, T), 1) // BLK == b).astype(F32).astype(BF16)
        total = total + jnp.dot(hit, spot, preferred_element_type=F32)
    chosen[...] = total


    lax.fori_loop(EARLY, R // 4, decode_four, 0)

    whole = qbuf.at[pl.ds(0, N - 1)]
    pltpu.make_async_copy(whole, whole, q_recv).wait()
    pltpu.make_async_copy(whole, whole, q_send).wait()
    to_row = iota((HD, HD), 0)
    to_col = iota((HD, HD), 1)
    origin = (to_col & 64) | ((to_col & 7) << 3) | ((to_col >> 3) & 7)
    permute = (to_row == origin).astype(F32).astype(BF16)
    for hh, (plain, turned) in enumerate(((qf0, qp0), (qf1, qp1))):
        part = qbuf[:, :, hh * HD : hh * HD + HD].reshape(N * R, HD)
        plain[: N * R, :] = part.astype(F32)
        turned[: N * R, :] = jnp.dot(part, permute, preferred_element_type=F32)

    all_keys.wait()
    all_vals.wait()
    left = (iota((16, 1), 0) & 7) < 4
    left_wide = (iota((16, HD), 0) & 7) < 4
    position = iota((1, T), 1) + me * T
    lane = iota((8, 128), 1)

    def spread_heads(part0, part1, r, p):
        at = pl.ds(p * 128 + r, 8, stride=16)
        both = jnp.concatenate([part0[at, :], part1[at, :]], axis=0)
        return jnp.concatenate(
            [jnp.where(left_wide, both, 0.0), jnp.where(left_wide, 0.0, both)], axis=1
        ).astype(BF16)

    def place(n):
        step = n // 4
        turn = jnp.where(lax.rem(me, 2) == 0, step + 1, 3 - step)
        return lax.rem(me // 8 + turn, PAIRS), lax.rem(n, 4) * 4

    def multiply(n):
        p, first = place(n)
        wide = pl.ds(pl.multiple_of(p * 256, 256), 256)
        for u in range(4):
            r = first + u
            at = slice(u * 16, u * 16 + 16)
            guesses[at, :] = jnp.dot(
                spread_heads(qp0, qp1, r, p), khat[r, wide, :], preferred_element_type=F32
            )
            scores[at, :] = lax.dot_general(
                spread_heads(qf0, qf1, r, p),
                keys[r, :, wide],
                (((1,), (1,)), ((), ())),
                preferred_element_type=F32,
            )

    def weigh(n):
        p, first = place(n)
        eight = pl.ds(pl.multiple_of(p * 8, 8), 8)
        kept = stat[eight, :]
        for u in range(4):
            r = first + u
            at = slice(u * 16, u * 16 + 16)
            inside = position < lens[r]
            guess = jnp.where(inside, guesses[at, :] * SCALE, NEGATIVE)
            guess_peak = jnp.max(guess, axis=1, keepdims=True)
            guess_total = jnp.sum(
                jnp.where(inside, jnp.exp(guess - guess_peak), 0.0), axis=1, keepdims=True
            )
            here = chosen[pl.ds(r * KVH + 2 * p, 1), :]
            there = chosen[pl.ds(r * KVH + 2 * p + 1, 1), :]
            used = (jnp.where(left, here, there) > 0.5) & inside
            score = jnp.where(used, scores[at, :] * SCALE, NEGATIVE)
            peak = jnp.max(score, axis=1, keepdims=True)
            weight = jnp.where(used, jnp.exp(score - peak), 0.0)
            weight_total = jnp.sum(weight, axis=1, keepdims=True)
            weights[at, :] = weight.astype(BF16)
            for kind, value in enumerate((guess_peak, guess_total, peak, weight_total)):
                for hh in range(2):
                    kept = jnp.where(
                        lane == kind * 32 + hh * 16 + r, value[hh * 8 : hh * 8 + 8], kept
                    )
        stat[eight, :] = kept

    def average(n):
        p, first = place(n)
        wide = pl.ds(pl.multiple_of(p * 256, 256), 256)
        for u in range(4):
            r = first + u
            summed = jnp.dot(
                weights[u * 16 : u * 16 + 16, :], vals[r, :, wide], preferred_element_type=F32
            )
            summed = jnp.where(left, summed[:, :HD], summed[:, HD:])
            stage[pl.ds(p * 256 + r, 8, stride=32), :] = summed[:8]
            stage[pl.ds(p * 256 + 16 + r, 8, stride=32), :] = summed[8:]

    def send_stats(n):
        p, _ = place(n)
        for k in range(8):
            stat_out[p * 8 + k] = stat[pl.ds(p * 8 + k, 1), :]

        def send_to(k, inner):
            to = p * 8 + lax.rem(me + 4 + k, 8)

            @pl.when(to != me)
            def _():
                pltpu.make_async_remote_copy(
                    src_ref=stat_out.at[to],
                    dst_ref=stat_in.at[me],
                    send_sem=s_send,
                    recv_sem=s_recv,
                    device_id={"ctx": to},
                    device_id_type=MESH,
                ).start()

            return inner

        lax.fori_loop(0, 8, send_to, 0)

    def send_values(n):
        p, _ = place(n)
        block = pl.ds(pl.multiple_of(p * 256, 256), 256)
        sendbuf[block, :] = stage[block, :].astype(BF16)

        def send_to(k, inner):
            to = p * 8 + lax.rem(me + 4 + k, 8)

            @pl.when(to != me)
            def _():
                pltpu.make_async_remote_copy(
                    src_ref=sendbuf.at[pl.ds(pl.multiple_of(to * 32, 32), 32)],
                    dst_ref=recvbuf.at[pl.ds(pl.multiple_of(me * 32, 32), 32)],
                    send_sem=o_send,
                    recv_sem=o_recv,
                    device_id={"ctx": to},
                    device_id_type=MESH,
                ).start()

            return inner

        lax.fori_loop(0, 8, send_to, 0)

    def send_both(n):
        p, _ = place(n)
        for k in range(8):
            stat_out[p * 8 + k] = stat[pl.ds(p * 8 + k, 1), :]
        block = pl.ds(pl.multiple_of(p * 256, 256), 256)
        sendbuf[block, :] = stage[block, :].astype(BF16)

        def send_to(k, inner):
            to = p * 8 + lax.rem(me + 4 + k, 8)

            @pl.when(to != me)
            def _():
                pltpu.make_async_remote_copy(
                    src_ref=stat_out.at[to],
                    dst_ref=stat_in.at[me],
                    send_sem=s_send,
                    recv_sem=s_recv,
                    device_id={"ctx": to},
                    device_id_type=MESH,
                ).start()
                pltpu.make_async_remote_copy(
                    src_ref=sendbuf.at[pl.ds(pl.multiple_of(to * 32, 32), 32)],
                    dst_ref=recvbuf.at[pl.ds(pl.multiple_of(me * 32, 32), 32)],
                    send_sem=o_send,
                    recv_sem=o_recv,
                    device_id={"ctx": to},
                    device_id_type=MESH,
                ).start()

            return inner

        lax.fori_loop(0, 8, send_to, 0)

    multiply(0)
    weigh(0)
    multiply(1)

    def attend(n, carry):
        average(n - 2)
        weigh(n - 1)
        multiply(n)

        @pl.when(lax.rem(n, 4) == 1)
        def _():
            send_both(n - 2)

        return carry

    lax.fori_loop(2, R, attend, 0)
    average(R - 2)
    weigh(R - 1)
    send_stats(R - 1)
    average(R - 1)
    send_values(R - 1)
    mine = pl.ds(pl.multiple_of(me * 32, 32), 32)
    recvbuf[mine, :] = sendbuf[mine, :]
    stat_in[me] = stat_out[me]

    source = iota((N, N * 32), 1) // 32
    spread = (source == iota((N, N * 32), 0)).astype(F32).astype(BF16)
    some = stat_in.at[pl.ds(0, N - 1)]
    pltpu.make_async_copy(some, some, s_recv).wait()
    stats = stat_in[...].reshape(N, 128)
    top = jnp.max(stats, axis=0, keepdims=True)
    factor = jnp.exp(stats - top)
    totals = jnp.sum(factor * pltpu.roll(stats, 96, 1), axis=0, keepdims=True)
    mass = top + jnp.log(totals)
    mass_ref[0:1, :] = mass[:, 0:16]
    mass_ref[1:2, :] = mass[:, 16:32]
    share = (factor / totals)[:, 64:96].T
    mix = jnp.dot(share.astype(BF16), spread, preferred_element_type=F32)
    same = (iota((32, N * 32), 1) & 31) == iota((32, N * 32), 0)
    mix = jnp.where(same, mix, 0.0).astype(BF16)
    some = recvbuf.at[pl.ds(0, (N - 1) * 32)]
    pltpu.make_async_copy(some, some, o_recv).wait()
    result = jnp.dot(mix, recvbuf[...], preferred_element_type=F32)
    att_ref[:, 0:HD] = result[:R].astype(BF16)
    att_ref[:, HD:] = result[R:].astype(BF16)
    some = stat_in.at[pl.ds(0, N - 1)]
    pltpu.make_async_copy(some, some, s_send).wait()
    some = recvbuf.at[pl.ds(0, (N - 1) * 32)]
    pltpu.make_async_copy(some, some, o_send).wait()


def body(queries, keys, values, codes, codebook, lengths, blocks):
    book = codebook.transpose(0, 1, 3, 2).reshape(KVH * M * 8, CODES)
    anywhere = pl.BlockSpec(memory_space=pl.ANY)
    vmem = pl.BlockSpec(memory_space=pltpu.VMEM)
    dma = pltpu.SemaphoreType.DMA
    attended, mass = pl.pallas_call(
        kernel,
        out_shape=(
            pltpu.VMEM((R, 2 * HD), BF16),
            pltpu.VMEM((2, R), F32),
        ),
        in_specs=[anywhere] * 7,
        out_specs=(vmem, vmem),
        scratch_shapes=[
            pltpu.VMEM((N, R, 2 * HD), BF16),
            pltpu.VMEM((N * R + 16, HD), F32),
            pltpu.VMEM((N * R + 16, HD), F32),
            pltpu.VMEM((N * R + 16, HD), F32),
            pltpu.VMEM((N * R + 16, HD), F32),
            pltpu.VMEM((R, T, KVH * M), jnp.int32),
            pltpu.VMEM((R, T, KVH * HD), BF16),
            pltpu.VMEM((R, T, KVH * HD), BF16),
            pltpu.VMEM((KVH * M * 8, CODES), BF16),
            pltpu.VMEM((KVH * M * 8 + 64, 128), F32),
            pltpu.VMEM((KVH * M * 8 + 64, 128), F32),
            pltpu.VMEM((KVH * M * 8, 128), F32),
            pltpu.VMEM((KVH * M * 8, 128), F32),
            pltpu.VMEM((R, KVH * HD, T), BF16),
            pltpu.SMEM((R,), jnp.int32),
            pltpu.VMEM((R, KVH, SEL), jnp.int32),
            pltpu.VMEM((R * KVH, T), F32),
            pltpu.VMEM((KVH * M, T), jnp.int32),
            pltpu.VMEM((KVH * M, T), jnp.int32),
            pltpu.VMEM((KVH * M, T), jnp.int32),
            pltpu.VMEM((KVH * M, T), jnp.int32),
            pltpu.VMEM((64, T), F32),
            pltpu.VMEM((64, T), F32),
            pltpu.VMEM((64, T), BF16),
            pltpu.VMEM((N * 32 + 32, HD), F32),
            pltpu.VMEM((N * 32, HD), BF16),
            pltpu.VMEM((N * 32, HD), BF16),
            pltpu.VMEM((N, 128), F32),
            pltpu.VMEM((N, 1, 128), F32),
            pltpu.VMEM((N, 1, 128), F32),
            pltpu.VMEM((R, 2 * HD), BF16),
            dma((4,)),
            dma((R // 2,)),
            dma, dma,
            dma, dma, dma, dma, dma, dma,
        ],
        compiler_params=pltpu.CompilerParams(
            collective_id=0, has_side_effects=True, vmem_limit_bytes=56 * 2**20
        ),
        name="decode_attention",
    )(queries, keys, values, codes, book, lengths, blocks)

    return attended, mass.T


def solution(mesh):
    placed = (
        P("rows", "ctx"),
        P("rows", "ctx", None),
        P("rows", "ctx", None),
        P("rows", "ctx", None),
        P(),
        P("rows"),
        P("rows", None, None),
    )
    return jax.shard_map(
        body,
        mesh=mesh,
        in_specs=placed,
        out_specs=(P("rows", "ctx"), P("rows", "ctx")),
        check_vma=False,
    )
```
